32 devices in a mesh: gx: 16 (over z, y, core), gy: 2 (over x).
Axes of the slice: x: 2, y: 2, z: 4, core: 2. Of those that a mesh axis runs over, the one named last changes fastest.
Arguments:
- conserved: float32 [5, 16, 128, 256], P(None, None, 'gx', 'gy'), may hold values from -2.5 to 9, as said below
- register: float32 [5, 16, 128, 256], P(None, None, 'gx', 'gy'), may hold values from -1 to 1, as said below
- ghost_planes: float32 [5, 16, 128, 256], P(None, None, 'gx', 'gy'), may hold values from -2.5 to 9, as said below
Outputs:
- advanced: float32 [5, 16, 128, 256], P(None, None, 'gx', 'gy')
- carried: float32 [5, 16, 128, 256], P(None, None, 'gx', 'gy')
The draws below stay inside these ranges and needn't reach their ends.
Inputs may be any that keep to these rules, and one draw needn't show every extreme that they name: `conserved`: every cell holds density in [0.6, 1.4], velocity components of magnitude at most 1.5 and T = 1.4 p / rho in [0.7, 1.4]; energy is E = p / 0.4 + 0.5 rho |u|^2. `ghost_planes`: every cell holds density in [0.6, 1.4], velocity components of magnitude at most 1.5 and T = 1.4 p / rho in [0.7, 1.4]; energy is E = p / 0.4 + 0.5 rho |u|^2. `register`: the density row lies in [-0.25, 0.25]; the momentum and energy rows lie in [-1, 1]. Density stays at 0.3 or more through both sections.
All inputs are finite; a program needn't handle non-finite values.
Results may differ from the reference program's by a relative error of at most 0.00002.
Values sent between devices are 32-bit elements; how exact they have to be, the bound alone decides.
A program may use at most 64 MiB of HBM per device.

```python
import math
import jax
import jax.numpy as jnp
from jax import lax

NZ = 16
GZ = 8
NX = 128
NY = 256


adiabatic_exponent = 1.4


def physical(key, planes):
    noise_seed_keys = jax.random.split(key, 4)
    lattice_shape_sizes = (planes, NX, NY)
    fluid_specific_weight = 0.6 * jnp.exp(jax.random.uniform(noise_seed_keys[0], lattice_shape_sizes, jnp.float32) * math.log(1.4 / 0.6))
    kelvin_scalar_field = jax.random.uniform(noise_seed_keys[2], lattice_shape_sizes, jnp.float32, 0.7, 1.4)
    fluid_speed_vector = jnp.clip(0.4 * jax.random.normal(noise_seed_keys[1], (3,) + lattice_shape_sizes, jnp.float32), -1.2, 1.2)
    static_stress_scalar = fluid_specific_weight * kelvin_scalar_field / adiabatic_exponent
    energy = static_stress_scalar / (adiabatic_exponent - 1.0) + 0.5 * fluid_specific_weight * (fluid_speed_vector[0] * fluid_speed_vector[0] + fluid_speed_vector[1] * fluid_speed_vector[1] + fluid_speed_vector[2] * fluid_speed_vector[2])
    return jnp.concatenate([fluid_specific_weight[None], fluid_specific_weight[None] * fluid_speed_vector, energy[None]], axis=0)


def draw_conserved(key, part):
    return physical(jax.random.fold_in(key, 11), NZ)


def draw_ghost_planes(key, part):
    return physical(jax.random.fold_in(key, 23), 2 * GZ)


def draw_register(key, part):
    noise_seed_keys = jax.random.split(jax.random.fold_in(key, 37), 2)
    lattice_shape_sizes = (NZ, NX, NY)
    density_row = jnp.clip(0.1 * jax.random.normal(noise_seed_keys[0], (1,) + lattice_shape_sizes, jnp.float32), -0.25, 0.25)
    other_rows = jnp.clip(0.3 * jax.random.normal(noise_seed_keys[1], (4,) + lattice_shape_sizes, jnp.float32), -1.0, 1.0)
    return jnp.concatenate([density_row, other_rows], axis=0)


def setup_inputs(seed: int = 0) -> dict:
    key_list = jax.random.split(jax.random.key(seed), 4)
    conserved = draw_conserved(jax.random.fold_in(key_list[3], 71), 0)
    register = draw_register(jax.random.fold_in(key_list[3], 71), 0)
    ghost_planes = draw_ghost_planes(jax.random.fold_in(key_list[3], 71), 0)
    return dict(conserved=conserved, register=register, ghost_planes=ghost_planes)


adiabatic_exponent = 1.4
viscosity = 0.15
conductivity = 0.15 / (0.4 * 0.7)
time_step = 0.2
section_a = (-0.41789047, -1.19215169)
section_b = (0.37921031, 0.82295503)
stencil = (0.8, -0.2, 4.0 / 105.0, -1.0 / 280.0)
slab_planes = 4


def derivative(field, along):
    extent = field.shape[along]
    result = None
    for offset, weight in enumerate(stencil, start=1):
        term = weight * (lax.slice_in_dim(field, 4 + offset, extent - 4 + offset, axis=along)
                         - lax.slice_in_dim(field, 4 - offset, extent - 4 - offset, axis=along))
        result = term if result is None else result + term
    return result


def roll_derivative(field, along):
    result = None
    for offset, weight in enumerate(stencil, start=1):
        term = weight * (jnp.roll(field, -offset, axis=along) - jnp.roll(field, offset, axis=along))
        result = term if result is None else result + term
    return result


def primitives(conserved):
    fluid_specific_weight = conserved[0]
    fluid_speed_vector = conserved[1:4] / fluid_specific_weight
    kinetic = 0.5 * fluid_specific_weight * (fluid_speed_vector[0] * fluid_speed_vector[0] + fluid_speed_vector[1] * fluid_speed_vector[1] + fluid_speed_vector[2] * fluid_speed_vector[2])
    static_stress_scalar = (adiabatic_exponent - 1.0) * (conserved[4] - kinetic)
    kelvin_scalar_field = adiabatic_exponent * static_stress_scalar / fluid_specific_weight
    return jnp.concatenate([fluid_speed_vector, kelvin_scalar_field[None], static_stress_scalar[None]], axis=0)


def euler_flux(conserved, primitive, direction):
    speed = primitive[direction]
    static_stress_scalar = primitive[4]
    entries = [conserved[1 + direction]]
    for index in range(3):
        entry = conserved[1 + index] * speed
        if index == direction:
            entry = entry + static_stress_scalar
        entries.append(entry)
    entries.append((conserved[4] + static_stress_scalar) * speed)
    return jnp.stack(entries, axis=0)


def viscous_flux(grads, primitive, direction):
    dilation = grads[0] + grads[4] + grads[8]
    stresses = []
    for index in range(3):
        stress = viscosity * (grads[3 * index + direction] + grads[3 * direction + index])
        if index == direction:
            stress = stress - (2.0 / 3.0) * viscosity * dilation
        stresses.append(stress)
    energy = (primitive[0] * stresses[0] + primitive[1] * stresses[1] + primitive[2] * stresses[2]
              + conductivity * grads[9 + direction])
    return jnp.stack(stresses + [energy], axis=0)


def net_flux(conserved, primitive, viscous, direction):
    inviscid = euler_flux(conserved, primitive, direction)
    return jnp.concatenate([inviscid[:1], inviscid[1:] - viscous], axis=0)


def slab_tendency(slab_cells):
    primitive = primitives(slab_cells)
    fields = primitive[:4]
    grad_x = roll_derivative(fields[:, 4:-4], 2)
    grad_y = roll_derivative(fields[:, 4:-4], 3)
    grad_z = derivative(fields, 1)
    grads = jnp.stack([grad_x, grad_y, grad_z], axis=1).reshape((12,) + grad_z.shape[1:])
    middle = grads[:, 4:-4]
    mid_prim = primitive[:, 8:-8]
    mid_cons = slab_cells[:, 8:-8]
    flux_x = net_flux(mid_cons, mid_prim, viscous_flux(middle, mid_prim, 0), 0)
    flux_y = net_flux(mid_cons, mid_prim, viscous_flux(middle, mid_prim, 1), 1)
    flux_z = net_flux(slab_cells[:, 4:-4], primitive[:, 4:-4], viscous_flux(grads, primitive[:, 4:-4], 2), 2)
    return -(roll_derivative(flux_x, 2) + roll_derivative(flux_y, 3) + derivative(flux_z, 1))


def reference(conserved, register, ghost_planes):
    current = conserved
    for step_index in range(2):
        extended = jnp.concatenate([ghost_planes[:, :GZ], current, ghost_planes[:, GZ:]], axis=1)
        firsts = jnp.arange(NZ // slab_planes, dtype=jnp.int32) * slab_planes

        def one_slab(first_plane):
            slab_cells = lax.dynamic_slice_in_dim(extended, first_plane, slab_planes + 16, axis=1)
            return slab_tendency(slab_cells)

        blocks = lax.map(one_slab, firsts)
        tendency = jnp.moveaxis(blocks, 0, 1).reshape((5, NZ, NX, NY))
        register = section_a[step_index] * register + time_step * tendency
        current = current + section_b[step_index] * register
    return current, register
```

```python
import functools

import jax
import jax.numpy as jnp
from jax import lax
from jax.experimental import pallas as pl
from jax.experimental.pallas import tpu as pltpu
from jax.sharding import PartitionSpec as P
import numpy as np

MESH = pl.DeviceIdType.MESH

viscosity = 0.15
conductivity = 0.15 / (0.4 * 0.7)
time_step = 0.2
section_a = (-0.41789047, -1.19215169)
section_b = (0.37921031, 0.82295503)
stencil = (0.8, -0.2, 4.0 / 105.0, -1.0 / 280.0)
coarse = [float(np.asarray(w, jnp.bfloat16)) for w in stencil]
fine = [w - c for w, c in zip(stencil, coarse, strict=True)]
CH = 4
HALF = CH // 2
GHOST = 8
SENT = HALF + 4 * CH
SLOTS = SENT + HALF
OWN = pl.ds(8, 8)
BEFORE = pl.ds(0, 8)
AFTER = pl.ds(16, 8)


def kernel(
    nx,
    ny,
    chunks,
    cons_hbm,
    reg_hbm,
    ghost_hbm,
    state_out,
    register_out,
    slope_out,
    QE,
    REG,
    XE,
    YP,
    YN,
    CP,
    CN,
    HH,
    XSG,
    XRG,
    DY,
    DZ,
    FX,
    FY,
    FZ,
    RS,
    GH,
    SD,
    ED,
    HE,
    HD,
    W,
    in_sem,
    xs_sem,
    xr_sem,
    ys_sem,
    yr_sem,
    ds_sem,
    dr_sem,
    gs_sem,
    gr_sem,
):
    ix = lax.axis_index("gx")
    iy = lax.axis_index("gy")
    beside = (lax.rem(ix + 1, nx), lax.rem(ix + nx - 1, nx))
    across = (lax.rem(iy + 1, ny), lax.rem(iy + ny - 1, ny))
    y_sides = (0,) if ny == 2 else (0, 1)

    planes = chunks * CH
    loads = [
        pltpu.make_async_copy(cons_hbm, QE.at[:, pl.ds(GHOST, planes)], in_sem.at[0]),
        pltpu.make_async_copy(ghost_hbm.at[:, pl.ds(0, GHOST)], QE.at[:, pl.ds(0, GHOST)], in_sem.at[1]),
        pltpu.make_async_copy(
            ghost_hbm.at[:, pl.ds(GHOST, GHOST)], QE.at[:, pl.ds(GHOST + planes, GHOST)], in_sem.at[2]
        ),
        pltpu.make_async_copy(reg_hbm, REG, in_sem.at[3]),
    ]
    for load in loads:
        load.start()

    barrier = pltpu.get_barrier_semaphore()
    neighbours = [{"gx": x} for x in beside]
    neighbours += [{"gy": across[way]} for way in y_sides]
    neighbours += [{"gx": x, "gy": across[way]} for x in beside for way in y_sides]
    for neighbour in neighbours:
        pl.semaphore_signal(barrier, inc=1, device_id=neighbour, device_id_type=MESH)

    sub = lax.broadcasted_iota(jnp.int32, (8, 128), 0)
    lane = lax.broadcasted_iota(jnp.int32, (8, 128), 1)
    low = sub < 4
    edge = jnp.logical_or(lane < 4, lane >= 124)
    first_half = lane < 64
    lane_half = lax.bitwise_and(lane, 63)
    lane_group = lax.shift_right_logical(lane_half, 4)
    late = lax.bitwise_and(lane, 15) >= 8
    own_lane = jnp.logical_xor(late, lane >= 64)

    def x_copy(way, s, c):
        slots = pl.ds((0, HALF)[way], SENT)
        return pltpu.make_async_remote_copy(
            src_ref=XE.at[s, c + 2, slots, OWN],
            dst_ref=XE.at[s, c + 2, slots, (BEFORE, AFTER)[way]],
            send_sem=xs_sem.at[way, s, c],
            recv_sem=xr_sem.at[way, s, c],
            device_id={"gx": beside[way]},
            device_id_type=MESH,
        )

    def y_copy(way, s, c):
        return pltpu.make_async_remote_copy(
            src_ref=YP.at[s, c + 1],
            dst_ref=YN.at[way, s, c + 1],
            send_sem=ys_sem.at[way, s, c],
            recv_sem=yr_sem.at[way, s, c],
            device_id={"gy": across[way]},
            device_id_type=MESH,
        )

    def d_copy(x_way, way, s, c):
        return pltpu.make_async_remote_copy(
            src_ref=CP.at[x_way, s, c],
            dst_ref=CN.at[way, x_way, s, c],
            send_sem=ds_sem.at[x_way, way, s, c],
            recv_sem=dr_sem.at[x_way, way, s, c],
            device_id={"gx": beside[x_way], "gy": across[way]},
            device_id_type=MESH,
        )

    def exchange(s, c):
        copies = [x_copy(way, s, c) for way in (0, 1)]
        copies += [d_copy(x_way, way, s, c) for x_way in (0, 1) for way in y_sides]
        return copies + [y_copy(way, s, c) for way in y_sides]

    def ghost_exchange():
        copies = []
        for way in (0, 1):
            copies.append(
                pltpu.make_async_remote_copy(
                    src_ref=XSG.at[way],
                    dst_ref=XRG.at[way],
                    send_sem=gs_sem.at[way],
                    recv_sem=gr_sem.at[way],
                    device_id={"gx": beside[way]},
                    device_id_type=MESH,
                )
            )
        for way in y_sides:
            for i, e in enumerate((0, chunks + 1)):
                copies.append(
                    pltpu.make_async_remote_copy(
                        src_ref=YP.at[0, e, pl.ds(1, 2)],
                        dst_ref=YN.at[way, 0, e, pl.ds(1, 2)],
                        send_sem=gs_sem.at[2 + 2 * way + i],
                        recv_sem=gr_sem.at[2 + 2 * way + i],
                        device_id={"gy": across[way]},
                        device_id_type=MESH,
                    )
                )
        return copies

    def pack_high(first, second):
        return jnp.where(low, pltpu.roll(second, 4, 0), first)

    def pack_low(first, second):
        return jnp.where(low, first, pltpu.roll(second, 4, 0))

    def unpack_x(from_left, from_right):
        first = jnp.where(low, from_right, from_left)
        second = pltpu.roll(jnp.where(low, from_left, from_right), 4, 0)
        return first, second

    def pack_y(items):
        packed = None
        for k, item in enumerate(items):
            turned = jnp.where(first_half, pltpu.roll(item, 16 * k + 8, 1), pltpu.roll(item, 16 * k + 72, 1))
            packed = turned if packed is None else jnp.where(lane_group == k, turned, packed)
        return packed

    def by_side(values):
        return values[0] if ny == 2 else jnp.where(first_half, values[0], values[1])

    def both_edges(strip):
        return jnp.where(late, strip, pltpu.roll(strip, 64, 1))

    def place(edges, k, inner):
        return jnp.where(edge, pltpu.roll(edges, 128 - (16 * k + 8), 1), inner)

    def add(edges, k, inner):
        return inner + jnp.where(edge, pltpu.roll(edges, 128 - (16 * k + 8), 1), 0.0)

    def weighted(pairs):
        total = None
        for weight, (plus, minus) in zip(stencil, pairs, strict=True):
            term = weight * (plus - minus)
            total = term if total is None else total + term
        return total

    def band(items):
        flat = jnp.concatenate(items, axis=0) if isinstance(items, list) else items.reshape(-1, 128)
        high = flat.astype(jnp.bfloat16)
        rest = (flat - high.astype(jnp.float32)).astype(jnp.bfloat16)
        out = jnp.dot(jnp.concatenate([high, rest], axis=1), W[...], preferred_element_type=jnp.float32)
        return (out[:, :128] + out[:, 128:]).reshape(-1, 8, 128)

    def d_rows(ref, index, start):
        return weighted(
            [(ref[index + (pl.ds(start + s, 8),)], ref[index + (pl.ds(start - s, 8),)]) for s in range(1, 5)]
        )

    def d_x(field, halo):
        return weighted(
            [
                (
                    pltpu.roll(jnp.where(sub < s, halo, field), 8 - s, 0),
                    pltpu.roll(jnp.where(sub >= 8 - s, halo, field), s, 0),
                )
                for s in range(1, 5)
            ]
        )

    def d_z(ref, f, z):
        return weighted([(ref[f, z + s], ref[f, z - s]) for s in range(1, 5)])

    def tile(s, c, f, k):
        return XE[s, c + k // CH, HALF + CH * f + k % CH, OWN]

    def d_z_tile(s, c, f, k):
        return weighted([(tile(s, c, f, k + o), tile(s, c, f, k - o)) for o in range(1, 5)])

    def d_z_strip(s, c, f):
        values = []
        for way in y_sides:
            before, here, after = [YN[way, s, c + i, f] for i in range(3)]
            pairs = [
                (
                    pltpu.roll(jnp.where(lane_half < 16 * o, after, here), 128 - 16 * o, 1),
                    pltpu.roll(jnp.where(lane_half >= 64 - 16 * o, before, here), 16 * o, 1),
                )
                for o in range(1, 4)
            ]
            values.append(weighted(pairs + [(after, before)]))
        return by_side(values)

    def primitives(q):
        inverse = 1.0 / q[0]
        speeds = [q[1] * inverse, q[2] * inverse, q[3] * inverse]
        kinetic = 0.5 * (q[1] * speeds[0] + q[2] * speeds[1] + q[3] * speeds[2])
        pressure = 0.4 * (q[4] - kinetic)
        return speeds + [1.4 * pressure * inverse]

    def thermal(rho, v):
        m = [rho * v[i] for i in range(3)]
        p = (1.0 / 1.4) * (rho * v[3])
        total = 3.5 * p + 0.5 * (m[0] * v[0] + m[1] * v[1] + m[2] * v[2])
        return m, p, total

    def flux(along, v, state, stress, gradient):
        m, p, total = state
        out = [m[along]]
        for i in range(3):
            entry = m[i] * v[along] - stress[i]
            out.append(entry + p if i == along else entry)
        work = v[0] * stress[0] + v[1] * stress[1] + v[2] * stress[2] + conductivity * gradient
        out.append(total * v[along] - work)
        return out

    def shrink(gx, gy, gz):
        return (2.0 / 3.0 * viscosity) * (gx + gy + gz)

    def put(s, c, values):
        for f in range(4):
            for k in range(CH):
                XE[s, c, HALF + CH * f + k, OWN] = values[k][f]

    def prepare(s, c, values, rho):
        put(s, c + 2, values)
        for j in range(HALF):
            XE[s, c + 2, j, OWN] = pack_high(rho[j], rho[j + HALF])
            XE[s, c + 2, SENT + j, OWN] = pack_low(rho[j], rho[j + HALF])
        packs = [pack_y([values[k][f] for k in range(CH)]) for f in range(4)] + [pack_y(rho)]
        for f in range(5):
            YP[s, c + 1, f] = packs[f]
        CP[0, s, c] = pack_high(packs[0], packs[1])
        CP[1, s, c] = pack_low(packs[0], packs[1])

    def start_chunk(c, carry):
        states = [[QE[f, GHOST + c * CH + k] for f in range(5)] for k in range(CH)]
        prepare(0, c, [primitives(q) for q in states], [q[0] for q in states])
        return carry

    def send_chunk(c, carry):
        for copy in exchange(0, c):
            copy.start()
        return carry

    def ghost_start():
        near = []
        for c in (0, 1, chunks + 2, chunks + 3):
            values = [primitives([QE[f, c * CH + k] for f in range(5)]) for k in range(CH)]
            for s in range(2):
                put(s, c, values)
            if c in (1, chunks + 2):
                near += values
                e = 0 if c == 1 else chunks + 1
                for f in (1, 2):
                    YP[0, e, f] = pack_y([values[k][f] for k in range(CH)])
        for i, f in enumerate((0, 2)):
            for k in range(4):
                XSG[0, i, k] = pack_high(near[k][f], near[k + 4][f])
                XSG[1, i, k] = pack_low(near[k][f], near[k + 4][f])

    def gradients_y(s):
        DY[...] = band(XE[s, pl.ds(2, chunks), pl.ds(HALF, 4 * CH), OWN]).reshape(DY.shape)

    def gradient_chunk(s, c, carry):
        for k in range(CH):
            for f in range(4):
                DZ[f, c * CH + k] = d_z_tile(s, c + 2, f, k)
        return carry

    def ghost_gradients():
        for copy in ghost_exchange():
            copy.wait_recv()
        sides = ((0, 0, 1), (chunks + 1, planes + 4, chunks + 2))
        items = []
        for e, _, c in sides:
            for f in (1, 2):
                for way in y_sides:
                    YN[way, 1, e, f] = YN[way, 0, e, f]
                merged = by_side([YN[way, 0, e, f] for way in y_sides])
                items.append(jnp.where(own_lane, YP[0, e, f], merged))
        for _, _, c in sides:
            items += [tile(0, c, f, k) for f in (1, 2) for k in range(CH)]
        out = band(items)
        for i, (_, at, c) in enumerate(sides):
            strips = [both_edges(out[2 * i + f]) for f in range(2)]
            inner = 4 + 2 * CH * i
            for k in range(CH):
                j = CH * i + k
                halos = []
                for n, f in enumerate((0, 2)):
                    halo = unpack_x(XRG[0, n, k], XRG[1, n, k])[i]
                    HH[f, at + k] = halo
                    halos.append(halo)
                GH[0, j] = d_x(tile(0, c, 0, k), halos[0]) + place(strips[0], k, out[inner + k])
                GH[1, j] = d_x(tile(0, c, 2, k), halos[1])
                GH[2, j] = place(strips[1], k, out[inner + CH + k])

    def ghost_flux(s):
        for e, at, c in ((0, 0, 1), (1, planes + 4, chunks + 2)):
            for k in range(CH):
                j = CH * e + k
                v = [tile(s, c, f, k) for f in range(4)]
                gz = [d_z_tile(s, c, f, k) for f in range(4)]
                dilation = (2.0 / 3.0 * viscosity) * (GH[0, j] + gz[2])
                stress = [
                    viscosity * (GH[1, j] + gz[0]),
                    viscosity * (GH[2, j] + gz[1]),
                    (2.0 * viscosity) * gz[2] - dilation,
                ]
                out = flux(2, v, thermal(QE[0, c * CH + k], v), stress, gz[3])
                for f in range(5):
                    FZ[f, at + k] = out[f]

    def beyond(s, c, f):
        return by_side([YN[way, s, c + 1, f] for way in y_sides])

    def corners(s, c):
        pairs = [unpack_x(CN[way, 0, s, c], CN[way, 1, s, c]) for way in y_sides]
        return [by_side([pair[f] for pair in pairs]) for f in range(2)]

    def arrive(s, c):
        for copy in exchange(s, c):
            copy.wait_recv()
        items = [jnp.where(own_lane, YP[s, c + 1, f], beyond(s, c, f)) for f in range(4)]
        items += [jnp.where(own_lane, 0.0, corner) for corner in corners(s, c)]
        for f in range(4):
            for k in range(CH):
                slot = HALF + CH * f + k
                halo = jnp.where(low, XE[s, c + 2, slot, AFTER], XE[s, c + 2, slot, BEFORE])
                HH[f, 4 + c * CH + k] = halo
                if f < 2:
                    items.append(halo)
        out = band(items)
        for f in range(4):
            SD[f, c] = out[f]
            ED[f, c] = both_edges(out[f])
        for f in range(2):
            HE[f, c] = both_edges(out[4 + f])
            for k in range(CH):
                HD[f, c * CH + k] = out[6 + CH * f + k]

    def strip_chunk(s, c):
        v = [beyond(s, c, f) for f in range(5)]
        strip_x = [d_x(v[f], corner) for f, corner in enumerate(corners(s, c))]
        strip_y = [SD[f, c] for f in range(4)]
        strip_z = [d_z_strip(s, c, f) for f in (1, 2)]
        dilation = shrink(strip_x[0], strip_y[1], strip_z[1])
        stress = [
            viscosity * (strip_x[1] + strip_y[0]),
            (2.0 * viscosity) * strip_y[1] - dilation,
            viscosity * (strip_y[2] + strip_z[0]),
        ]
        out = flux(1, v, thermal(v[4], v), stress, strip_y[3])
        out = band([jnp.where(own_lane, 0.0, out[min(f, 4)]) for f in range(6)])
        for f in range(5):
            RS[f, c] = both_edges(out[f])

    def flux_chunk(s, c):
        halo_rho = [None] * CH
        for j in range(HALF):
            halo_rho[j], halo_rho[j + HALF] = unpack_x(XE[s, c + 2, j, BEFORE], XE[s, c + 2, SENT + j, AFTER])
        for k in range(CH):
            w = c * CH + k
            gx = []
            halo_gx = []
            for f in range(4):
                index = (s, c + 2, HALF + CH * f + k)
                lower = d_rows(XE, index, 4)
                upper = d_rows(XE, index, 12)
                gx.append(pltpu.roll(jnp.where(low, upper, lower), 4, 0))
                halo_gx.append(pltpu.roll(jnp.where(low, lower, upper), 4, 0))

            v = [HH[f, 4 + w] for f in range(4)]
            gy = [add(HE[f, c], k, HD[f, w]) for f in range(2)]
            gz = [d_z(HH, f, 4 + w) for f in (0, 2)]
            dilation = shrink(halo_gx[0], gy[1], gz[1])
            stress = [
                (2.0 * viscosity) * halo_gx[0] - dilation,
                viscosity * (halo_gx[1] + gy[0]),
                viscosity * (halo_gx[2] + gz[0]),
            ]
            out = flux(0, v, thermal(halo_rho[k], v), stress, halo_gx[3])
            for f in range(5):
                FX[f, w, BEFORE] = out[f]
                FX[f, w, AFTER] = out[f]

            v = [tile(s, c + 2, f, k) for f in range(4)]
            state = thermal(QE[0, GHOST + w], v)
            gy = [place(ED[f, c], k, DY[c, CH * f + k]) for f in range(4)]
            gz = [DZ[f, w] for f in range(4)]
            dilation = shrink(gx[0], gy[1], gz[2])
            txx = (2.0 * viscosity) * gx[0] - dilation
            tyy = (2.0 * viscosity) * gy[1] - dilation
            tzz = (2.0 * viscosity) * gz[2] - dilation
            txy = viscosity * (gx[1] + gy[0])
            txz = viscosity * (gx[2] + gz[0])
            tyz = viscosity * (gy[2] + gz[1])
            out_x = flux(0, v, state, [txx, txy, txz], gx[3])
            out_y = flux(1, v, state, [txy, tyy, tyz], gy[3])
            out_z = flux(2, v, state, [txz, tyz, tzz], gz[3])
            for f in range(5):
                FX[f, w, OWN] = out_x[f]
                FY[c, CH * f + k] = out_y[f]
                FZ[f, w + 4] = out_z[f]

    def update_chunk(s, c):
        inner = band(FY[c])
        values = []
        rho = []
        for k in range(CH):
            w = c * CH + k
            z = GHOST + w
            q = []
            for f in range(5):
                slope = d_rows(FX, (f, w), 8) + add(RS[f, c], k, inner[CH * f + k]) + d_z(FZ, f, w + 4)
                if s == 1:
                    slope_out[f, w] = slope
                    continue
                register = section_a[0] * REG[f, w] - time_step * slope
                register_out[f, w] = register
                state = QE[f, z] + section_b[0] * register
                QE[f, z] = state
                state_out[f, w] = state
                q.append(state)
            if s == 0:
                values.append(primitives(q))
                rho.append(q[0])
        if s == 0:
            prepare(1, c, values, rho)
            for copy in exchange(1, c):
                copy.start()

    def step(s, c, carry):
        @pl.when(c + 2 < chunks)
        def _():
            arrive(s, c + 2)

        @pl.when(c + 1 < chunks)
        def _():
            strip_chunk(s, c + 1)
            flux_chunk(s, c + 1)

        @pl.when(c >= 0)
        def _():
            update_chunk(s, c)

        return carry

    offset = lax.broadcasted_iota(jnp.int32, (128, 128), 0) - lax.broadcasted_iota(jnp.int32, (128, 128), 1)
    distance = jnp.abs(offset)
    for weights, part in ((coarse, pl.ds(0, 128)), (fine, pl.ds(128, 128))):
        taps = jnp.zeros((128, 128), jnp.float32)
        for o, weight in enumerate(weights, start=1):
            taps = jnp.where(distance == o, weight, taps)
        taps = jnp.where(offset < 0, -taps, taps).astype(jnp.bfloat16)
        W[pl.ds(0, 128), part] = taps
        W[pl.ds(128, 128), part] = taps

    loads[0].wait()
    lax.fori_loop(0, chunks, start_chunk, 0)
    loads[1].wait()
    loads[2].wait()
    ghost_start()
    pl.semaphore_wait(barrier, len(neighbours))
    for copy in ghost_exchange():
        copy.start()
    lax.fori_loop(0, chunks, send_chunk, 0)
    for s in range(2):
        gradients_y(s)
        lax.fori_loop(0, chunks, functools.partial(gradient_chunk, s), 0)
        if s == 0:
            ghost_gradients()
            loads[3].wait()
        ghost_flux(s)
        arrive(s, 0)
        lax.fori_loop(-1, chunks, functools.partial(step, s), 0)

    for copy in ghost_exchange():
        copy.wait_send()

    def finish(c, carry):
        for s in range(2):
            for copy in exchange(s, c):
                copy.wait_send()
        return carry

    lax.fori_loop(0, chunks, finish, 0)


def solution(mesh):
    nx, ny = mesh.shape["gx"], mesh.shape["gy"]
    sides = 1 if ny == 2 else 2

    def body(conserved, register, ghost_planes):
        _, planes, rows, columns = conserved.shape
        assert (rows, columns) == (8, 128) and planes % CH == 0 and ghost_planes.shape[1] == 2 * GHOST
        chunks = planes // CH

        def vmem(*shape, rows=8):
            return pltpu.VMEM(shape + (rows, columns), jnp.float32)

        dma = pltpu.SemaphoreType.DMA
        state, old, slope = pl.pallas_call(
            functools.partial(kernel, nx, ny, chunks),
            out_shape=[pltpu.VMEM(conserved.shape, jnp.float32)] * 3,
            in_specs=[pl.BlockSpec(memory_space=pltpu.HBM)] * 3,
            out_specs=[pl.BlockSpec(memory_space=pltpu.VMEM)] * 3,
            scratch_shapes=[
                vmem(5, planes + 2 * GHOST),
                vmem(5, planes),
                vmem(2, chunks + 4, SLOTS, rows=24),
                vmem(2, chunks + 2, 5),
                vmem(sides, 2, chunks + 2, 5),
                vmem(2, 2, chunks),
                vmem(sides, 2, 2, chunks),
                vmem(4, planes + 8),
                vmem(2, 2, 4),
                vmem(2, 2, 4),
                vmem(chunks, 4 * CH),
                vmem(4, planes),
                vmem(5, planes, rows=24),
                vmem(chunks, 5 * CH),
                vmem(5, planes + 8),
                vmem(5, chunks),
                vmem(3, 8),
                vmem(4, chunks),
                vmem(4, chunks),
                vmem(2, chunks),
                vmem(2, planes),
                pltpu.VMEM((256, 256), jnp.bfloat16),
                dma((4,)),
                dma((2, 2, chunks)),
                dma((2, 2, chunks)),
                dma((sides, 2, chunks)),
                dma((sides, 2, chunks)),
                dma((2, sides, 2, chunks)),
                dma((2, sides, 2, chunks)),
                dma((2 + 2 * sides,)),
                dma((2 + 2 * sides,)),
            ],
            compiler_params=pltpu.CompilerParams(
                collective_id=0, has_side_effects=True, vmem_limit_bytes=60 * 1024 * 1024
            ),
        )(conserved, register, ghost_planes)
        carried = section_a[1] * old - time_step * slope
        return state + section_b[1] * carried, carried

    spec = P(None, None, "gx", "gy")
    return jax.shard_map(
        body, mesh=mesh, in_specs=(spec, spec, spec), out_specs=(spec, spec), check_vma=False
    )
```

```python
import functools

import jax
import jax.numpy as jnp
from jax import lax
from jax.experimental import pallas as pl
from jax.experimental.pallas import tpu as pltpu
from jax.sharding import PartitionSpec as P
import numpy as np

MESH = pl.DeviceIdType.MESH

viscosity = 0.15
conductivity = 0.15 / (0.4 * 0.7)
time_step = 0.2
section_a = (-0.41789047, -1.19215169)
section_b = (0.37921031, 0.82295503)
stencil = (0.8, -0.2, 4.0 / 105.0, -1.0 / 280.0)
coarse = [float(np.asarray(w, jnp.bfloat16)) for w in stencil]
fine = [w - c for w, c in zip(stencil, coarse, strict=True)]
CH = 4
HALF = CH // 2
GHOST = 8
SENT = HALF + 4 * CH
SLOTS = SENT + HALF
OWN = pl.ds(8, 8)
BEFORE = pl.ds(0, 8)
AFTER = pl.ds(16, 8)


def kernel(
    nx,
    ny,
    chunks,
    cons_hbm,
    reg_hbm,
    ghost_hbm,
    state_out,
    register_out,
    slope_out,
    QE,
    REG,
    XE,
    YP,
    YN,
    CP,
    CN,
    HH,
    XSG,
    XRG,
    DY,
    DZ,
    FX,
    FY,
    FZ,
    RS,
    GH,
    SD,
    ED,
    HE,
    HD,
    HX,
    W,
    in_sem,
    xs_sem,
    xr_sem,
    ys_sem,
    yr_sem,
    ds_sem,
    dr_sem,
    gs_sem,
    gr_sem,
):
    ix = lax.axis_index("gx")
    iy = lax.axis_index("gy")
    beside = (lax.rem(ix + 1, nx), lax.rem(ix + nx - 1, nx))
    across = (lax.rem(iy + 1, ny), lax.rem(iy + ny - 1, ny))
    y_sides = (0,) if ny == 2 else (0, 1)

    planes = chunks * CH
    loads = [
        pltpu.make_async_copy(cons_hbm, QE.at[:, pl.ds(GHOST, planes)], in_sem.at[0]),
        pltpu.make_async_copy(ghost_hbm.at[:, pl.ds(0, GHOST)], QE.at[:, pl.ds(0, GHOST)], in_sem.at[1]),
        pltpu.make_async_copy(
            ghost_hbm.at[:, pl.ds(GHOST, GHOST)], QE.at[:, pl.ds(GHOST + planes, GHOST)], in_sem.at[2]
        ),
        pltpu.make_async_copy(reg_hbm, REG, in_sem.at[3]),
    ]
    for load in loads:
        load.start()

    barrier = pltpu.get_barrier_semaphore()
    neighbours = [{"gx": x} for x in beside]
    neighbours += [{"gy": across[way]} for way in y_sides]
    neighbours += [{"gx": x, "gy": across[way]} for x in beside for way in y_sides]
    for neighbour in neighbours:
        pl.semaphore_signal(barrier, inc=1, device_id=neighbour, device_id_type=MESH)

    sub = lax.broadcasted_iota(jnp.int32, (8, 128), 0)
    lane = lax.broadcasted_iota(jnp.int32, (8, 128), 1)
    low = sub < 4
    edge = jnp.logical_or(lane < 4, lane >= 124)
    first_half = lane < 64
    lane_half = lax.bitwise_and(lane, 63)
    lane_group = lax.shift_right_logical(lane_half, 4)
    late = lax.bitwise_and(lane, 15) >= 8
    own_lane = jnp.logical_xor(late, lane >= 64)

    def x_copy(way, s, c):
        slots = pl.ds((0, HALF)[way], SENT)
        return pltpu.make_async_remote_copy(
            src_ref=XE.at[s, c + 2, slots, OWN],
            dst_ref=XE.at[s, c + 2, slots, (BEFORE, AFTER)[way]],
            send_sem=xs_sem.at[way, s, c],
            recv_sem=xr_sem.at[way, s, c],
            device_id={"gx": beside[way]},
            device_id_type=MESH,
        )

    def y_copy(way, s, c):
        return pltpu.make_async_remote_copy(
            src_ref=YP.at[s, c + 1],
            dst_ref=YN.at[way, s, c + 1],
            send_sem=ys_sem.at[way, s, c],
            recv_sem=yr_sem.at[way, s, c],
            device_id={"gy": across[way]},
            device_id_type=MESH,
        )

    def d_copy(x_way, way, s, c):
        return pltpu.make_async_remote_copy(
            src_ref=CP.at[x_way, s, c],
            dst_ref=CN.at[way, x_way, s, c],
            send_sem=ds_sem.at[x_way, way, s, c],
            recv_sem=dr_sem.at[x_way, way, s, c],
            device_id={"gx": beside[x_way], "gy": across[way]},
            device_id_type=MESH,
        )

    def exchange(s, c):
        copies = [x_copy(way, s, c) for way in (0, 1)]
        copies += [d_copy(x_way, way, s, c) for x_way in (0, 1) for way in y_sides]
        return copies + [y_copy(way, s, c) for way in y_sides]

    def ghost_exchange():
        copies = []
        for way in (0, 1):
            copies.append(
                pltpu.make_async_remote_copy(
                    src_ref=XSG.at[way],
                    dst_ref=XRG.at[way],
                    send_sem=gs_sem.at[way],
                    recv_sem=gr_sem.at[way],
                    device_id={"gx": beside[way]},
                    device_id_type=MESH,
                )
            )
        for way in y_sides:
            for i, e in enumerate((0, chunks + 1)):
                copies.append(
                    pltpu.make_async_remote_copy(
                        src_ref=YP.at[0, e, pl.ds(1, 2)],
                        dst_ref=YN.at[way, 0, e, pl.ds(1, 2)],
                        send_sem=gs_sem.at[2 + 2 * way + i],
                        recv_sem=gr_sem.at[2 + 2 * way + i],
                        device_id={"gy": across[way]},
                        device_id_type=MESH,
                    )
                )
        return copies

    def pack_high(first, second):
        return jnp.where(low, pltpu.roll(second, 4, 0), first)

    def pack_low(first, second):
        return jnp.where(low, first, pltpu.roll(second, 4, 0))

    def unpack_x(from_left, from_right):
        first = jnp.where(low, from_right, from_left)
        second = pltpu.roll(jnp.where(low, from_left, from_right), 4, 0)
        return first, second

    def pack_y(items):
        packed = None
        for k, item in enumerate(items):
            turned = jnp.where(first_half, pltpu.roll(item, 16 * k + 8, 1), pltpu.roll(item, 16 * k + 72, 1))
            packed = turned if packed is None else jnp.where(lane_group == k, turned, packed)
        return packed

    def by_side(values):
        return values[0] if ny == 2 else jnp.where(first_half, values[0], values[1])

    def both_edges(strip):
        return jnp.where(late, strip, pltpu.roll(strip, 64, 1))

    def place(edges, k, inner):
        return jnp.where(edge, pltpu.roll(edges, 128 - (16 * k + 8), 1), inner)

    def add(edges, k, inner):
        return inner + jnp.where(edge, pltpu.roll(edges, 128 - (16 * k + 8), 1), 0.0)

    def weighted(pairs):
        total = None
        for weight, (plus, minus) in zip(stencil, pairs, strict=True):
            term = weight * (plus - minus)
            total = term if total is None else total + term
        return total

    def band(items):
        flat = jnp.concatenate(items, axis=0) if isinstance(items, list) else items.reshape(-1, 128)
        high = flat.astype(jnp.bfloat16)
        rest = (flat - high.astype(jnp.float32)).astype(jnp.bfloat16)
        out = jnp.dot(jnp.concatenate([high, rest], axis=1), W[...], preferred_element_type=jnp.float32)
        return (out[:, :128] + out[:, 128:]).reshape(-1, 8, 128)

    def d_rows(ref, index, start):
        return weighted(
            [(ref[index + (pl.ds(start + s, 8),)], ref[index + (pl.ds(start - s, 8),)]) for s in range(1, 5)]
        )

    def d_x(field, halo):
        return weighted(
            [
                (
                    pltpu.roll(jnp.where(sub < s, halo, field), 8 - s, 0),
                    pltpu.roll(jnp.where(sub >= 8 - s, halo, field), s, 0),
                )
                for s in range(1, 5)
            ]
        )

    def d_z(ref, f, z):
        return weighted([(ref[f, z + s], ref[f, z - s]) for s in range(1, 5)])

    def tile(s, c, f, k):
        return XE[s, c + k // CH, HALF + CH * f + k % CH, OWN]

    def d_z_tile(s, c, f, k):
        return weighted([(tile(s, c, f, k + o), tile(s, c, f, k - o)) for o in range(1, 5)])

    def d_z_strip(s, c, f):
        values = []
        for way in y_sides:
            before, here, after = [YN[way, s, c + i, f] for i in range(3)]
            pairs = [
                (
                    pltpu.roll(jnp.where(lane_half < 16 * o, after, here), 128 - 16 * o, 1),
                    pltpu.roll(jnp.where(lane_half >= 64 - 16 * o, before, here), 16 * o, 1),
                )
                for o in range(1, 4)
            ]
            values.append(weighted(pairs + [(after, before)]))
        return by_side(values)

    def primitives(q):
        inverse = 1.0 / q[0]
        speeds = [q[1] * inverse, q[2] * inverse, q[3] * inverse]
        kinetic = 0.5 * (q[1] * speeds[0] + q[2] * speeds[1] + q[3] * speeds[2])
        pressure = 0.4 * (q[4] - kinetic)
        return speeds + [1.4 * pressure * inverse]

    def thermal(rho, v):
        m = [rho * v[i] for i in range(3)]
        p = (1.0 / 1.4) * (rho * v[3])
        total = 3.5 * p + 0.5 * (m[0] * v[0] + m[1] * v[1] + m[2] * v[2])
        return m, p, total

    def flux(along, v, state, stress, gradient):
        m, p, total = state
        out = [m[along]]
        for i in range(3):
            entry = m[i] * v[along] - stress[i]
            out.append(entry + p if i == along else entry)
        work = v[0] * stress[0] + v[1] * stress[1] + v[2] * stress[2] + conductivity * gradient
        out.append(total * v[along] - work)
        return out

    def shrink(gx, gy, gz):
        return (2.0 / 3.0 * viscosity) * (gx + gy + gz)

    def put(s, c, values):
        for f in range(4):
            for k in range(CH):
                XE[s, c, HALF + CH * f + k, OWN] = values[k][f]

    def prepare(s, c, values, rho):
        put(s, c + 2, values)
        for j in range(HALF):
            XE[s, c + 2, j, OWN] = pack_high(rho[j], rho[j + HALF])
            XE[s, c + 2, SENT + j, OWN] = pack_low(rho[j], rho[j + HALF])
        packs = [pack_y([values[k][f] for k in range(CH)]) for f in range(4)] + [pack_y(rho)]
        for f in range(5):
            YP[s, c + 1, f] = packs[f]
        CP[0, s, c] = pack_high(packs[0], packs[1])
        CP[1, s, c] = pack_low(packs[0], packs[1])

    def start_chunk(c, carry):
        states = [[QE[f, GHOST + c * CH + k] for f in range(5)] for k in range(CH)]
        prepare(0, c, [primitives(q) for q in states], [q[0] for q in states])
        return carry

    def send_chunk(c, carry):
        for copy in exchange(0, c):
            copy.start()
        return carry

    def ghost_start():
        near = []
        for c in (0, 1, chunks + 2, chunks + 3):
            values = [primitives([QE[f, c * CH + k] for f in range(5)]) for k in range(CH)]
            for s in range(2):
                put(s, c, values)
            if c in (1, chunks + 2):
                near += values
                e = 0 if c == 1 else chunks + 1
                for f in (1, 2):
                    YP[0, e, f] = pack_y([values[k][f] for k in range(CH)])
        for i, f in enumerate((0, 2)):
            for k in range(4):
                XSG[0, i, k] = pack_high(near[k][f], near[k + 4][f])
                XSG[1, i, k] = pack_low(near[k][f], near[k + 4][f])

    def gradients_y(s):
        DY[...] = band(XE[s, pl.ds(2, chunks), pl.ds(HALF, 4 * CH), OWN]).reshape(DY.shape)

    def gradient_chunk(s, c, carry):
        for k in range(CH):
            for f in range(4):
                DZ[f, c * CH + k] = d_z_tile(s, c + 2, f, k)
        return carry

    def ghost_gradients():
        for copy in ghost_exchange():
            copy.wait_recv()
        sides = ((0, 0, 1), (chunks + 1, planes + 4, chunks + 2))
        items = []
        for e, _, c in sides:
            for f in (1, 2):
                for way in y_sides:
                    YN[way, 1, e, f] = YN[way, 0, e, f]
                merged = by_side([YN[way, 0, e, f] for way in y_sides])
                items.append(jnp.where(own_lane, YP[0, e, f], merged))
        for _, _, c in sides:
            items += [tile(0, c, f, k) for f in (1, 2) for k in range(CH)]
        out = band(items)
        for i, (_, at, c) in enumerate(sides):
            strips = [both_edges(out[2 * i + f]) for f in range(2)]
            inner = 4 + 2 * CH * i
            for k in range(CH):
                j = CH * i + k
                halos = []
                for n, f in enumerate((0, 2)):
                    halo = unpack_x(XRG[0, n, k], XRG[1, n, k])[i]
                    HH[f, at + k] = halo
                    halos.append(halo)
                GH[0, j] = d_x(tile(0, c, 0, k), halos[0]) + place(strips[0], k, out[inner + k])
                GH[1, j] = d_x(tile(0, c, 2, k), halos[1])
                GH[2, j] = place(strips[1], k, out[inner + CH + k])

    def ghost_flux(s):
        for e, at, c in ((0, 0, 1), (1, planes + 4, chunks + 2)):
            for k in range(CH):
                j = CH * e + k
                v = [tile(s, c, f, k) for f in range(4)]
                gz = [d_z_tile(s, c, f, k) for f in range(4)]
                dilation = (2.0 / 3.0 * viscosity) * (GH[0, j] + gz[2])
                stress = [
                    viscosity * (GH[1, j] + gz[0]),
                    viscosity * (GH[2, j] + gz[1]),
                    (2.0 * viscosity) * gz[2] - dilation,
                ]
                out = flux(2, v, thermal(QE[0, c * CH + k], v), stress, gz[3])
                for f in range(5):
                    FZ[f, at + k] = out[f]

    def beyond(s, c, f):
        return by_side([YN[way, s, c + 1, f] for way in y_sides])

    def corners(s, c):
        pairs = [unpack_x(CN[way, 0, s, c], CN[way, 1, s, c]) for way in y_sides]
        return [by_side([pair[f] for pair in pairs]) for f in range(2)]

    def arrive(s, c):
        for copy in exchange(s, c):
            copy.wait_recv()
        items = [jnp.where(own_lane, YP[s, c + 1, f], beyond(s, c, f)) for f in range(4)]
        items += [jnp.where(own_lane, 0.0, corner) for corner in corners(s, c)]
        for f in range(4):
            for k in range(CH):
                slot = HALF + CH * f + k
                halo = jnp.where(low, XE[s, c + 2, slot, AFTER], XE[s, c + 2, slot, BEFORE])
                HH[f, 4 + c * CH + k] = halo
                if f < 2:
                    items.append(halo)
        out = band(items)
        for f in range(4):
            SD[f, c] = out[f]
            ED[f, c] = both_edges(out[f])
        for f in range(2):
            HE[f, c] = both_edges(out[4 + f])
            for k in range(CH):
                HD[f, c * CH + k] = out[6 + CH * f + k]

    def strip_chunk(s, c):
        v = [beyond(s, c, f) for f in range(5)]
        strip_x = [d_x(v[f], corner) for f, corner in enumerate(corners(s, c))]
        strip_y = [SD[f, c] for f in range(4)]
        strip_z = [d_z_strip(s, c, f) for f in (1, 2)]
        dilation = shrink(strip_x[0], strip_y[1], strip_z[1])
        stress = [
            viscosity * (strip_x[1] + strip_y[0]),
            (2.0 * viscosity) * strip_y[1] - dilation,
            viscosity * (strip_y[2] + strip_z[0]),
        ]
        out = flux(1, v, thermal(v[4], v), stress, strip_y[3])
        out = band([jnp.where(own_lane, 0.0, out[min(f, 4)]) for f in range(6)])
        for f in range(5):
            RS[f, c] = both_edges(out[f])

    def halo_chunk(s, c):
        rho = [None] * CH
        for j in range(HALF):
            rho[j], rho[j + HALF] = unpack_x(XE[s, c + 2, j, BEFORE], XE[s, c + 2, SENT + j, AFTER])
        for k in range(CH):
            w = c * CH + k
            v = [HH[f, 4 + w] for f in range(4)]
            gx = [HX[f, w] for f in range(4)]
            gy = [add(HE[f, c], k, HD[f, w]) for f in range(2)]
            gz = [d_z(HH, f, 4 + w) for f in (0, 2)]
            dilation = shrink(gx[0], gy[1], gz[1])
            stress = [
                (2.0 * viscosity) * gx[0] - dilation,
                viscosity * (gx[1] + gy[0]),
                viscosity * (gx[2] + gz[0]),
            ]
            out = flux(0, v, thermal(rho[k], v), stress, gx[3])
            for f in range(5):
                FX[f, w, BEFORE] = out[f]
                FX[f, w, AFTER] = out[f]

    def flux_chunk(s, c):
        for k in range(CH):
            w = c * CH + k
            gx = []
            for f in range(4):
                index = (s, c + 2, HALF + CH * f + k)
                lower = d_rows(XE, index, 4)
                upper = d_rows(XE, index, 12)
                gx.append(pltpu.roll(jnp.where(low, upper, lower), 4, 0))
                HX[f, w] = pltpu.roll(jnp.where(low, lower, upper), 4, 0)
            v = [tile(s, c + 2, f, k) for f in range(4)]
            state = thermal(QE[0, GHOST + w], v)
            gy = [place(ED[f, c], k, DY[c, CH * f + k]) for f in range(4)]
            gz = [DZ[f, w] for f in range(4)]
            dilation = shrink(gx[0], gy[1], gz[2])
            txx = (2.0 * viscosity) * gx[0] - dilation
            tyy = (2.0 * viscosity) * gy[1] - dilation
            tzz = (2.0 * viscosity) * gz[2] - dilation
            txy = viscosity * (gx[1] + gy[0])
            txz = viscosity * (gx[2] + gz[0])
            tyz = viscosity * (gy[2] + gz[1])
            out_x = flux(0, v, state, [txx, txy, txz], gx[3])
            out_y = flux(1, v, state, [txy, tyy, tyz], gy[3])
            out_z = flux(2, v, state, [txz, tyz, tzz], gz[3])
            for f in range(5):
                FX[f, w, OWN] = out_x[f]
                FY[c, CH * f + k] = out_y[f]
                FZ[f, w + 4] = out_z[f]

    def update_chunk(s, c):
        inner = band(FY[c])
        values = []
        rho = []
        for k in range(CH):
            w = c * CH + k
            z = GHOST + w
            q = []
            for f in range(5):
                slope = d_rows(FX, (f, w), 8) + add(RS[f, c], k, inner[CH * f + k]) + d_z(FZ, f, w + 4)
                if s == 1:
                    slope_out[f, w] = slope
                    continue
                register = section_a[0] * REG[f, w] - time_step * slope
                register_out[f, w] = register
                state = QE[f, z] + section_b[0] * register
                QE[f, z] = state
                state_out[f, w] = state
                q.append(state)
            if s == 0:
                values.append(primitives(q))
                rho.append(q[0])
        if s == 0:
            prepare(1, c, values, rho)
            for copy in exchange(1, c):
                copy.start()

    def step(s, c):
        if c + 1 < chunks:
            arrive(s, c + 1)
            flux_chunk(s, c + 1)
        if c >= 0:
            strip_chunk(s, c)
            halo_chunk(s, c)
            update_chunk(s, c)

    offset = lax.broadcasted_iota(jnp.int32, (128, 128), 0) - lax.broadcasted_iota(jnp.int32, (128, 128), 1)
    distance = jnp.abs(offset)
    for weights, part in ((coarse, pl.ds(0, 128)), (fine, pl.ds(128, 128))):
        taps = jnp.zeros((128, 128), jnp.float32)
        for o, weight in enumerate(weights, start=1):
            taps = jnp.where(distance == o, weight, taps)
        taps = jnp.where(offset < 0, -taps, taps).astype(jnp.bfloat16)
        W[pl.ds(0, 128), part] = taps
        W[pl.ds(128, 128), part] = taps

    loads[0].wait()
    for c in range(chunks):
        start_chunk(c, 0)
    loads[1].wait()
    loads[2].wait()
    ghost_start()
    pl.semaphore_wait(barrier, len(neighbours))
    for copy in ghost_exchange():
        copy.start()
    lax.fori_loop(0, chunks, send_chunk, 0)
    for s in range(2):
        gradients_y(s)
        for c in range(chunks):
            gradient_chunk(s, c, 0)
        if s == 0:
            ghost_gradients()
            loads[3].wait()
        ghost_flux(s)
        for c in range(-1, chunks):
            step(s, c)

    for copy in ghost_exchange():
        copy.wait_send()

    def finish(c, carry):
        for s in range(2):
            for copy in exchange(s, c):
                copy.wait_send()
        return carry

    lax.fori_loop(0, chunks, finish, 0)


def solution(mesh):
    nx, ny = mesh.shape["gx"], mesh.shape["gy"]
    sides = 1 if ny == 2 else 2

    def body(conserved, register, ghost_planes):
        _, planes, rows, columns = conserved.shape
        assert (rows, columns) == (8, 128) and planes % CH == 0 and ghost_planes.shape[1] == 2 * GHOST
        chunks = planes // CH

        def vmem(*shape, rows=8):
            return pltpu.VMEM(shape + (rows, columns), jnp.float32)

        dma = pltpu.SemaphoreType.DMA
        state, old, slope = pl.pallas_call(
            functools.partial(kernel, nx, ny, chunks),
            out_shape=[pltpu.VMEM(conserved.shape, jnp.float32)] * 3,
            in_specs=[pl.BlockSpec(memory_space=pltpu.HBM)] * 3,
            out_specs=[pl.BlockSpec(memory_space=pltpu.VMEM)] * 3,
            scratch_shapes=[
                vmem(5, planes + 2 * GHOST),
                vmem(5, planes),
                vmem(2, chunks + 4, SLOTS, rows=24),
                vmem(2, chunks + 2, 5),
                vmem(sides, 2, chunks + 2, 5),
                vmem(2, 2, chunks),
                vmem(sides, 2, 2, chunks),
                vmem(4, planes + 8),
                vmem(2, 2, 4),
                vmem(2, 2, 4),
                vmem(chunks, 4 * CH),
                vmem(4, planes),
                vmem(5, planes, rows=24),
                vmem(chunks, 5 * CH),
                vmem(5, planes + 8),
                vmem(5, chunks),
                vmem(3, 8),
                vmem(4, chunks),
                vmem(4, chunks),
                vmem(2, chunks),
                vmem(2, planes),
                vmem(4, planes),
                pltpu.VMEM((256, 256), jnp.bfloat16),
                dma((4,)),
                dma((2, 2, chunks)),
                dma((2, 2, chunks)),
                dma((sides, 2, chunks)),
                dma((sides, 2, chunks)),
                dma((2, sides, 2, chunks)),
                dma((2, sides, 2, chunks)),
                dma((2 + 2 * sides,)),
                dma((2 + 2 * sides,)),
            ],
            compiler_params=pltpu.CompilerParams(
                collective_id=0, has_side_effects=True, vmem_limit_bytes=60 * 1024 * 1024
            ),
        )(conserved, register, ghost_planes)
        carried = section_a[1] * old - time_step * slope
        return state + section_b[1] * carried, carried

    spec = P(None, None, "gx", "gy")
    return jax.shard_map(
        body, mesh=mesh, in_specs=(spec, spec, spec), out_specs=(spec, spec), check_vma=False
    )
```

```python
import functools

import jax
import jax.numpy as jnp
from jax import lax
from jax.experimental import pallas as pl
from jax.experimental.pallas import tpu as pltpu
from jax.sharding import PartitionSpec as P
import numpy as np

MESH = pl.DeviceIdType.MESH

viscosity = 0.15
conductivity = 0.15 / (0.4 * 0.7)
time_step = 0.2
section_a = (-0.41789047, -1.19215169)
section_b = (0.37921031, 0.82295503)
stencil = (0.8, -0.2, 4.0 / 105.0, -1.0 / 280.0)
coarse = [float(np.asarray(w, jnp.bfloat16)) for w in stencil]
fine = [w - c for w, c in zip(stencil, coarse, strict=True)]
CH = 4
HALF = CH // 2
GHOST = 8
SENT = HALF + 4 * CH
SLOTS = SENT + HALF
OWN = pl.ds(8, 8)
BEFORE = pl.ds(0, 8)
AFTER = pl.ds(16, 8)


def kernel(
    nx,
    ny,
    chunks,
    cons_hbm,
    reg_hbm,
    ghost_hbm,
    state_out,
    register_out,
    slope_out,
    QE,
    REG,
    XE,
    YP,
    YN,
    CP,
    CN,
    HH,
    XSG,
    XRG,
    DY,
    DZ,
    FX,
    FY,
    FZ,
    RS,
    GH,
    SD,
    ED,
    HE,
    HD,
    HX,
    W,
    in_sem,
    xs_sem,
    xr_sem,
    ys_sem,
    yr_sem,
    ds_sem,
    dr_sem,
    gs_sem,
    gr_sem,
):
    ix = lax.axis_index("gx")
    iy = lax.axis_index("gy")
    beside = (lax.rem(ix + 1, nx), lax.rem(ix + nx - 1, nx))
    across = (lax.rem(iy + 1, ny), lax.rem(iy + ny - 1, ny))
    y_sides = (0,) if ny == 2 else (0, 1)

    planes = chunks * CH
    loads = [
        pltpu.make_async_copy(ghost_hbm.at[:, pl.ds(0, GHOST)], QE.at[:, pl.ds(0, GHOST)], in_sem.at[1]),
        pltpu.make_async_copy(
            ghost_hbm.at[:, pl.ds(GHOST, GHOST)], QE.at[:, pl.ds(GHOST + planes, GHOST)], in_sem.at[2]
        ),
        pltpu.make_async_copy(cons_hbm, QE.at[:, pl.ds(GHOST, planes)], in_sem.at[0]),
        pltpu.make_async_copy(reg_hbm, REG, in_sem.at[3]),
    ]
    for load in loads:
        load.start()

    barrier = pltpu.get_barrier_semaphore()
    neighbours = [{"gx": x} for x in beside]
    neighbours += [{"gy": across[way]} for way in y_sides]
    neighbours += [{"gx": x, "gy": across[way]} for x in beside for way in y_sides]
    for neighbour in neighbours:
        pl.semaphore_signal(barrier, inc=1, device_id=neighbour, device_id_type=MESH)

    sub = lax.broadcasted_iota(jnp.int32, (8, 128), 0)
    lane = lax.broadcasted_iota(jnp.int32, (8, 128), 1)
    low = sub < 4
    edge = jnp.logical_or(lane < 4, lane >= 124)
    first_half = lane < 64
    lane_half = lax.bitwise_and(lane, 63)
    lane_group = lax.shift_right_logical(lane_half, 4)
    late = lax.bitwise_and(lane, 15) >= 8
    own_lane = jnp.logical_xor(late, lane >= 64)

    def x_copy(way, s, c):
        slots = pl.ds((0, HALF)[way], SENT)
        return pltpu.make_async_remote_copy(
            src_ref=XE.at[s, c + 2, slots, OWN],
            dst_ref=XE.at[s, c + 2, slots, (BEFORE, AFTER)[way]],
            send_sem=xs_sem.at[way, s, c],
            recv_sem=xr_sem.at[way, s, c],
            device_id={"gx": beside[way]},
            device_id_type=MESH,
        )

    def y_copy(way, s, c):
        return pltpu.make_async_remote_copy(
            src_ref=YP.at[s, c + 1],
            dst_ref=YN.at[way, s, c + 1],
            send_sem=ys_sem.at[way, s, c],
            recv_sem=yr_sem.at[way, s, c],
            device_id={"gy": across[way]},
            device_id_type=MESH,
        )

    def d_copy(x_way, way, s, c):
        return pltpu.make_async_remote_copy(
            src_ref=CP.at[x_way, s, c],
            dst_ref=CN.at[way, x_way, s, c],
            send_sem=ds_sem.at[x_way, way, s, c],
            recv_sem=dr_sem.at[x_way, way, s, c],
            device_id={"gx": beside[x_way], "gy": across[way]},
            device_id_type=MESH,
        )

    def exchange(s, c):
        copies = [d_copy(x_way, way, s, c) for x_way in (0, 1) for way in y_sides]
        copies += [y_copy(way, s, c) for way in y_sides]
        return copies + [x_copy(way, s, c) for way in (0, 1)]

    def ghost_exchange():
        copies = []
        for way in (0, 1):
            copies.append(
                pltpu.make_async_remote_copy(
                    src_ref=XSG.at[way],
                    dst_ref=XRG.at[way],
                    send_sem=gs_sem.at[way],
                    recv_sem=gr_sem.at[way],
                    device_id={"gx": beside[way]},
                    device_id_type=MESH,
                )
            )
        for way in y_sides:
            for i, e in enumerate((0, chunks + 1)):
                copies.append(
                    pltpu.make_async_remote_copy(
                        src_ref=YP.at[0, e, pl.ds(1, 2)],
                        dst_ref=YN.at[way, 0, e, pl.ds(1, 2)],
                        send_sem=gs_sem.at[2 + 2 * way + i],
                        recv_sem=gr_sem.at[2 + 2 * way + i],
                        device_id={"gy": across[way]},
                        device_id_type=MESH,
                    )
                )
        return copies

    def pack_high(first, second):
        return jnp.where(low, pltpu.roll(second, 4, 0), first)

    def pack_low(first, second):
        return jnp.where(low, first, pltpu.roll(second, 4, 0))

    def unpack_x(from_left, from_right):
        first = jnp.where(low, from_right, from_left)
        second = pltpu.roll(jnp.where(low, from_left, from_right), 4, 0)
        return first, second

    def pack_y(items):
        packed = None
        for k, item in enumerate(items):
            turned = jnp.where(first_half, pltpu.roll(item, 16 * k + 8, 1), pltpu.roll(item, 16 * k + 72, 1))
            packed = turned if packed is None else jnp.where(lane_group == k, turned, packed)
        return packed

    def by_side(values):
        return values[0] if ny == 2 else jnp.where(first_half, values[0], values[1])

    def both_edges(strip):
        return jnp.where(late, strip, pltpu.roll(strip, 64, 1))

    def place(edges, k, inner):
        return jnp.where(edge, pltpu.roll(edges, 128 - (16 * k + 8), 1), inner)

    def add(edges, k, inner):
        return inner + jnp.where(edge, pltpu.roll(edges, 128 - (16 * k + 8), 1), 0.0)

    def weighted(pairs):
        total = None
        for weight, (plus, minus) in zip(stencil, pairs, strict=True):
            term = weight * (plus - minus)
            total = term if total is None else total + term
        return total

    def band(items):
        flat = jnp.concatenate(items, axis=0) if isinstance(items, list) else items.reshape(-1, 128)
        high = flat.astype(jnp.bfloat16)
        rest = (flat - high.astype(jnp.float32)).astype(jnp.bfloat16)
        out = jnp.dot(jnp.concatenate([high, rest], axis=1), W[...], preferred_element_type=jnp.float32)
        return (out[:, :128] + out[:, 128:]).reshape(-1, 8, 128)

    def d_rows(ref, index, start):
        return weighted(
            [(ref[index + (pl.ds(start + s, 8),)], ref[index + (pl.ds(start - s, 8),)]) for s in range(1, 5)]
        )

    def d_x(field, halo):
        return weighted(
            [
                (
                    pltpu.roll(jnp.where(sub < s, halo, field), 8 - s, 0),
                    pltpu.roll(jnp.where(sub >= 8 - s, halo, field), s, 0),
                )
                for s in range(1, 5)
            ]
        )

    def d_z(ref, f, z):
        return weighted([(ref[f, z + s], ref[f, z - s]) for s in range(1, 5)])

    def tile(s, c, f, k):
        return XE[s, c + k // CH, HALF + CH * f + k % CH, OWN]

    def d_z_tile(s, c, f, k):
        return weighted([(tile(s, c, f, k + o), tile(s, c, f, k - o)) for o in range(1, 5)])

    def d_z_strip(s, c, f):
        values = []
        for way in y_sides:
            before, here, after = [YN[way, s, c + i, f] for i in range(3)]
            pairs = [
                (
                    pltpu.roll(jnp.where(lane_half < 16 * o, after, here), 128 - 16 * o, 1),
                    pltpu.roll(jnp.where(lane_half >= 64 - 16 * o, before, here), 16 * o, 1),
                )
                for o in range(1, 4)
            ]
            values.append(weighted(pairs + [(after, before)]))
        return by_side(values)

    def primitives(q):
        inverse = 1.0 / q[0]
        speeds = [q[1] * inverse, q[2] * inverse, q[3] * inverse]
        kinetic = 0.5 * (q[1] * speeds[0] + q[2] * speeds[1] + q[3] * speeds[2])
        pressure = 0.4 * (q[4] - kinetic)
        return speeds + [1.4 * pressure * inverse]

    def thermal(rho, v):
        m = [rho * v[i] for i in range(3)]
        p = (1.0 / 1.4) * (rho * v[3])
        total = 3.5 * p + 0.5 * (m[0] * v[0] + m[1] * v[1] + m[2] * v[2])
        return m, p, total

    def flux(along, v, state, stress, gradient):
        m, p, total = state
        out = [m[along]]
        for i in range(3):
            entry = m[i] * v[along] - stress[i]
            out.append(entry + p if i == along else entry)
        work = v[0] * stress[0] + v[1] * stress[1] + v[2] * stress[2] + conductivity * gradient
        out.append(total * v[along] - work)
        return out

    def shrink(gx, gy, gz):
        return (2.0 / 3.0 * viscosity) * (gx + gy + gz)

    def put(s, c, values):
        for f in range(4):
            for k in range(CH):
                XE[s, c, HALF + CH * f + k, OWN] = values[k][f]

    def prepare(s, c, values, rho):
        put(s, c + 2, values)
        for j in range(HALF):
            XE[s, c + 2, j, OWN] = pack_high(rho[j], rho[j + HALF])
            XE[s, c + 2, SENT + j, OWN] = pack_low(rho[j], rho[j + HALF])
        packs = [pack_y([values[k][f] for k in range(CH)]) for f in range(4)] + [pack_y(rho)]
        for f in range(5):
            YP[s, c + 1, f] = packs[f]
        corner = jnp.where(first_half, packs[0], packs[1])
        CP[0, s, c] = corner[4:]
        CP[1, s, c] = corner[:4]

    def start_chunk(c, carry):
        states = [[QE[f, GHOST + c * CH + k] for f in range(5)] for k in range(CH)]
        prepare(0, c, [primitives(q) for q in states], [q[0] for q in states])
        return carry

    def send_chunk(c, carry):
        for copy in exchange(0, c):
            copy.start()
        return carry

    def ghost_primitives(c):
        values = [primitives([QE[f, c * CH + k] for f in range(5)]) for k in range(CH)]
        for s in range(2):
            put(s, c, values)
        return values

    def ghost_start():
        near = []
        for e, c in ((0, 1), (chunks + 1, chunks + 2)):
            values = ghost_primitives(c)
            near += values
            for f in (1, 2):
                YP[0, e, f] = pack_y([values[k][f] for k in range(CH)])
        for i, f in enumerate((0, 2)):
            for k in range(4):
                XSG[0, i, k] = pack_high(near[k][f], near[k + 4][f])
                XSG[1, i, k] = pack_low(near[k][f], near[k + 4][f])

    def gradients_y(s):
        DY[...] = band(XE[s, pl.ds(2, chunks), pl.ds(HALF, 4 * CH), OWN]).reshape(DY.shape)

    def gradient_chunk(s, c, carry):
        for k in range(CH):
            for f in range(4):
                DZ[f, c * CH + k] = d_z_tile(s, c + 2, f, k)
        return carry

    def ghost_gradients():
        for copy in ghost_exchange():
            copy.wait_recv()
        sides = ((0, 0, 1), (chunks + 1, planes + 4, chunks + 2))
        items = []
        for e, _, c in sides:
            for f in (1, 2):
                for way in y_sides:
                    YN[way, 1, e, f] = YN[way, 0, e, f]
                merged = by_side([YN[way, 0, e, f] for way in y_sides])
                items.append(jnp.where(own_lane, YP[0, e, f], merged))
        for _, _, c in sides:
            items += [tile(0, c, f, k) for f in (1, 2) for k in range(CH)]
        out = band(items)
        for i, (_, at, c) in enumerate(sides):
            strips = [both_edges(out[2 * i + f]) for f in range(2)]
            inner = 4 + 2 * CH * i
            for k in range(CH):
                j = CH * i + k
                halos = []
                for n, f in enumerate((0, 2)):
                    halo = unpack_x(XRG[0, n, k], XRG[1, n, k])[i]
                    HH[f, at + k] = halo
                    halos.append(halo)
                GH[0, j] = d_x(tile(0, c, 0, k), halos[0]) + place(strips[0], k, out[inner + k])
                GH[1, j] = d_x(tile(0, c, 2, k), halos[1])
                GH[2, j] = place(strips[1], k, out[inner + CH + k])

    def ghost_flux(s):
        for e, at, c in ((0, 0, 1), (1, planes + 4, chunks + 2)):
            for k in range(CH):
                j = CH * e + k
                v = [tile(s, c, f, k) for f in range(4)]
                gz = [d_z_tile(s, c, f, k) for f in range(4)]
                dilation = (2.0 / 3.0 * viscosity) * (GH[0, j] + gz[2])
                stress = [
                    viscosity * (GH[1, j] + gz[0]),
                    viscosity * (GH[2, j] + gz[1]),
                    (2.0 * viscosity) * gz[2] - dilation,
                ]
                out = flux(2, v, thermal(QE[0, c * CH + k], v), stress, gz[3])
                for f in range(5):
                    FZ[f, at + k] = out[f]

    def beyond(s, c, f):
        return by_side([YN[way, s, c + 1, f] for way in y_sides])

    def corners(s, c):
        pairs = [jnp.concatenate([CN[way, 1, s, c], CN[way, 0, s, c]], axis=0) for way in y_sides]
        turned = [pltpu.roll(pair, 64, 1) for pair in pairs]
        first = [jnp.where(first_half, pair, turn) for pair, turn in zip(pairs, turned, strict=True)]
        second = [jnp.where(first_half, turn, pair) for pair, turn in zip(pairs, turned, strict=True)]
        return [by_side(first), by_side(second)]

    def arrive(s, c):
        for copy in exchange(s, c):
            copy.wait_recv()
        items = [jnp.where(own_lane, YP[s, c + 1, f], beyond(s, c, f)) for f in range(4)]
        items += [jnp.where(own_lane, 0.0, corner) for corner in corners(s, c)]
        for f in range(4):
            for k in range(CH):
                slot = HALF + CH * f + k
                halo = jnp.where(low, XE[s, c + 2, slot, AFTER], XE[s, c + 2, slot, BEFORE])
                HH[f, 4 + c * CH + k] = halo
                if f < 2:
                    items.append(halo)
        out = band(items)
        for f in range(4):
            SD[f, c] = out[f]
            ED[f, c] = both_edges(out[f])
        for f in range(2):
            HE[f, c] = both_edges(out[4 + f])
            for k in range(CH):
                HD[f, c * CH + k] = out[6 + CH * f + k]

    def strip_chunk(s, c):
        v = [beyond(s, c, f) for f in range(5)]
        strip_x = [d_x(v[f], corner) for f, corner in enumerate(corners(s, c))]
        strip_y = [SD[f, c] for f in range(4)]
        strip_z = [d_z_strip(s, c, f) for f in (1, 2)]
        dilation = shrink(strip_x[0], strip_y[1], strip_z[1])
        stress = [
            viscosity * (strip_x[1] + strip_y[0]),
            (2.0 * viscosity) * strip_y[1] - dilation,
            viscosity * (strip_y[2] + strip_z[0]),
        ]
        out = flux(1, v, thermal(v[4], v), stress, strip_y[3])
        out = band([jnp.where(own_lane, 0.0, out[min(f, 4)]) for f in range(6)])
        for f in range(5):
            RS[f, c] = both_edges(out[f])

    def halo_chunk(s, c):
        rho = [None] * CH
        for j in range(HALF):
            rho[j], rho[j + HALF] = unpack_x(XE[s, c + 2, j, BEFORE], XE[s, c + 2, SENT + j, AFTER])
        for k in range(CH):
            w = c * CH + k
            v = [HH[f, 4 + w] for f in range(4)]
            gx = [HX[f, w] for f in range(4)]
            gy = [add(HE[f, c], k, HD[f, w]) for f in range(2)]
            gz = [d_z(HH, f, 4 + w) for f in (0, 2)]
            dilation = shrink(gx[0], gy[1], gz[1])
            stress = [
                (2.0 * viscosity) * gx[0] - dilation,
                viscosity * (gx[1] + gy[0]),
                viscosity * (gx[2] + gz[0]),
            ]
            out = flux(0, v, thermal(rho[k], v), stress, gx[3])
            for f in range(5):
                FX[f, w, BEFORE] = out[f]
                FX[f, w, AFTER] = out[f]

    def flux_chunk(s, c):
        for k in range(CH):
            w = c * CH + k
            gx = []
            for f in range(4):
                index = (s, c + 2, HALF + CH * f + k)
                lower = d_rows(XE, index, 4)
                upper = d_rows(XE, index, 12)
                gx.append(pltpu.roll(jnp.where(low, upper, lower), 4, 0))
                HX[f, w] = pltpu.roll(jnp.where(low, lower, upper), 4, 0)
            v = [tile(s, c + 2, f, k) for f in range(4)]
            state = thermal(QE[0, GHOST + w], v)
            gy = [place(ED[f, c], k, DY[c, CH * f + k]) for f in range(4)]
            gz = [DZ[f, w] for f in range(4)]
            dilation = shrink(gx[0], gy[1], gz[2])
            txx = (2.0 * viscosity) * gx[0] - dilation
            tyy = (2.0 * viscosity) * gy[1] - dilation
            tzz = (2.0 * viscosity) * gz[2] - dilation
            txy = viscosity * (gx[1] + gy[0])
            txz = viscosity * (gx[2] + gz[0])
            tyz = viscosity * (gy[2] + gz[1])
            out_x = flux(0, v, state, [txx, txy, txz], gx[3])
            out_y = flux(1, v, state, [txy, tyy, tyz], gy[3])
            out_z = flux(2, v, state, [txz, tyz, tzz], gz[3])
            for f in range(5):
                FX[f, w, OWN] = out_x[f]
                FY[c, CH * f + k] = out_y[f]
                FZ[f, w + 4] = out_z[f]

    def update_chunk(s, c):
        inner = band(FY[c])
        values = []
        rho = []
        for k in range(CH):
            w = c * CH + k
            z = GHOST + w
            q = []
            for f in range(5):
                slope = d_rows(FX, (f, w), 8) + add(RS[f, c], k, inner[CH * f + k]) + d_z(FZ, f, w + 4)
                if s == 1:
                    slope_out[f, w] = slope
                    continue
                register = section_a[0] * REG[f, w] - time_step * slope
                register_out[f, w] = register
                state = QE[f, z] + section_b[0] * register
                QE[f, z] = state
                state_out[f, w] = state
                q.append(state)
            if s == 0:
                values.append(primitives(q))
                rho.append(q[0])
        if s == 0:
            prepare(1, c, values, rho)
            for copy in exchange(1, c):
                copy.start()

    def step(s, c):
        if c + 1 < chunks:
            arrive(s, c + 1)
            flux_chunk(s, c + 1)
        if c >= 0:
            strip_chunk(s, c)
            halo_chunk(s, c)
            update_chunk(s, c)

    offset = lax.broadcasted_iota(jnp.int32, (128, 128), 0) - lax.broadcasted_iota(jnp.int32, (128, 128), 1)
    distance = jnp.abs(offset)
    for weights, part in ((coarse, pl.ds(0, 128)), (fine, pl.ds(128, 128))):
        taps = jnp.zeros((128, 128), jnp.float32)
        for o, weight in enumerate(weights, start=1):
            taps = jnp.where(distance == o, weight, taps)
        taps = jnp.where(offset < 0, -taps, taps).astype(jnp.bfloat16)
        W[pl.ds(0, 128), part] = taps
        W[pl.ds(128, 128), part] = taps

    loads[0].wait()
    loads[1].wait()
    ghost_start()
    loads[2].wait()
    start_chunk(0, 0)
    pl.semaphore_wait(barrier, len(neighbours))
    for copy in ghost_exchange():
        copy.start()
    send_chunk(0, 0)
    for c in range(1, chunks):
        start_chunk(c, 0)
        send_chunk(c, 0)
    ghost_primitives(0)
    ghost_primitives(chunks + 3)
    for s in range(2):
        gradients_y(s)
        for c in range(chunks):
            gradient_chunk(s, c, 0)
        if s == 0:
            ghost_gradients()
            loads[3].wait()
        ghost_flux(s)
        for c in range(-1, chunks):
            step(s, c)

    for copy in ghost_exchange():
        copy.wait_send()

    def finish(c, carry):
        for s in range(2):
            for copy in exchange(s, c):
                copy.wait_send()
        return carry

    lax.fori_loop(0, chunks, finish, 0)


def solution(mesh):
    nx, ny = mesh.shape["gx"], mesh.shape["gy"]
    sides = 1 if ny == 2 else 2

    def body(conserved, register, ghost_planes):
        _, planes, rows, columns = conserved.shape
        assert (rows, columns) == (8, 128) and planes % CH == 0 and ghost_planes.shape[1] == 2 * GHOST
        chunks = planes // CH

        def vmem(*shape, rows=8):
            return pltpu.VMEM(shape + (rows, columns), jnp.float32)

        dma = pltpu.SemaphoreType.DMA
        state, old, slope = pl.pallas_call(
            functools.partial(kernel, nx, ny, chunks),
            out_shape=[pltpu.VMEM(conserved.shape, jnp.float32)] * 3,
            in_specs=[pl.BlockSpec(memory_space=pltpu.HBM)] * 3,
            out_specs=[pl.BlockSpec(memory_space=pltpu.VMEM)] * 3,
            scratch_shapes=[
                vmem(5, planes + 2 * GHOST),
                vmem(5, planes),
                vmem(2, chunks + 4, SLOTS, rows=24),
                vmem(2, chunks + 2, 5),
                vmem(sides, 2, chunks + 2, 5),
                vmem(2, 2, chunks, rows=4),
                vmem(sides, 2, 2, chunks, rows=4),
                vmem(4, planes + 8),
                vmem(2, 2, 4),
                vmem(2, 2, 4),
                vmem(chunks, 4 * CH),
                vmem(4, planes),
                vmem(5, planes, rows=24),
                vmem(chunks, 5 * CH),
                vmem(5, planes + 8),
                vmem(5, chunks),
                vmem(3, 8),
                vmem(4, chunks),
                vmem(4, chunks),
                vmem(2, chunks),
                vmem(2, planes),
                vmem(4, planes),
                pltpu.VMEM((256, 256), jnp.bfloat16),
                dma((4,)),
                dma((2, 2, chunks)),
                dma((2, 2, chunks)),
                dma((sides, 2, chunks)),
                dma((sides, 2, chunks)),
                dma((2, sides, 2, chunks)),
                dma((2, sides, 2, chunks)),
                dma((2 + 2 * sides,)),
                dma((2 + 2 * sides,)),
            ],
            compiler_params=pltpu.CompilerParams(
                collective_id=0, has_side_effects=True, vmem_limit_bytes=60 * 1024 * 1024
            ),
        )(conserved, register, ghost_planes)
        carried = section_a[1] * old - time_step * slope
        return state + section_b[1] * carried, carried

    spec = P(None, None, "gx", "gy")
    return jax.shard_map(
        body, mesh=mesh, in_specs=(spec, spec, spec), out_specs=(spec, spec), check_vma=False
    )
```

```python
import functools

import jax
import jax.numpy as jnp
from jax import lax
from jax.experimental import pallas as pl
from jax.experimental.pallas import tpu as pltpu
from jax.sharding import PartitionSpec as P
import numpy as np

MESH = pl.DeviceIdType.MESH

viscosity = 0.15
conductivity = 0.15 / (0.4 * 0.7)
time_step = 0.2
section_a = (-0.41789047, -1.19215169)
section_b = (0.37921031, 0.82295503)
stencil = (0.8, -0.2, 4.0 / 105.0, -1.0 / 280.0)
coarse = [float(np.asarray(w, jnp.bfloat16)) for w in stencil]
fine = [w - c for w, c in zip(stencil, coarse, strict=True)]
CH = 4
HALF = CH // 2
GHOST = 8
SENT = HALF + 4 * CH
SLOTS = SENT + HALF
OWN = pl.ds(8, 8)
BEFORE = pl.ds(0, 8)
AFTER = pl.ds(16, 8)


def kernel(
    nx,
    ny,
    chunks,
    cons_hbm,
    reg_hbm,
    ghost_hbm,
    state_out,
    slope_out,
    QE,
    REG,
    XE,
    YP,
    YN,
    CP,
    CN,
    HH,
    XSG,
    XRG,
    DY,
    DZ,
    FX,
    FY,
    FZ,
    RS,
    GH,
    SD,
    ED,
    HE,
    HD,
    HX,
    W,
    in_sem,
    xs_sem,
    xr_sem,
    ys_sem,
    yr_sem,
    ds_sem,
    dr_sem,
    gs_sem,
    gr_sem,
):
    ix = lax.axis_index("gx")
    iy = lax.axis_index("gy")
    beside = (lax.rem(ix + 1, nx), lax.rem(ix + nx - 1, nx))
    across = (lax.rem(iy + 1, ny), lax.rem(iy + ny - 1, ny))
    y_sides = (0,) if ny == 2 else (0, 1)

    planes = chunks * CH
    loads = [
        pltpu.make_async_copy(ghost_hbm.at[:, pl.ds(0, GHOST)], QE.at[:, pl.ds(0, GHOST)], in_sem.at[1]),
        pltpu.make_async_copy(
            ghost_hbm.at[:, pl.ds(GHOST, GHOST)], QE.at[:, pl.ds(GHOST + planes, GHOST)], in_sem.at[2]
        ),
        pltpu.make_async_copy(cons_hbm, QE.at[:, pl.ds(GHOST, planes)], in_sem.at[0]),
        pltpu.make_async_copy(reg_hbm, REG, in_sem.at[3]),
    ]
    for load in loads:
        load.start()

    barrier = pltpu.get_barrier_semaphore()
    neighbours = [{"gx": x} for x in beside]
    neighbours += [{"gy": across[way]} for way in y_sides]
    neighbours += [{"gx": x, "gy": across[way]} for x in beside for way in y_sides]
    for neighbour in neighbours:
        pl.semaphore_signal(barrier, inc=1, device_id=neighbour, device_id_type=MESH)

    sub = lax.broadcasted_iota(jnp.int32, (8, 128), 0)
    lane = lax.broadcasted_iota(jnp.int32, (8, 128), 1)
    low = sub < 4
    edge = jnp.logical_or(lane < 4, lane >= 124)
    first_half = lane < 64
    lane_half = lax.bitwise_and(lane, 63)
    lane_group = lax.shift_right_logical(lane_half, 4)
    late = lax.bitwise_and(lane, 15) >= 8
    own_lane = jnp.logical_xor(late, lane >= 64)

    def x_copy(way, s, c):
        slots = pl.ds((0, HALF)[way], SENT)
        return pltpu.make_async_remote_copy(
            src_ref=XE.at[s, c + 2, slots, OWN],
            dst_ref=XE.at[s, c + 2, slots, (BEFORE, AFTER)[way]],
            send_sem=xs_sem.at[way, s, c],
            recv_sem=xr_sem.at[way, s, c],
            device_id={"gx": beside[way]},
            device_id_type=MESH,
        )

    def y_copy(way, s, c):
        return pltpu.make_async_remote_copy(
            src_ref=YP.at[s, c + 1],
            dst_ref=YN.at[way, s, c + 1],
            send_sem=ys_sem.at[way, s, c],
            recv_sem=yr_sem.at[way, s, c],
            device_id={"gy": across[way]},
            device_id_type=MESH,
        )

    def d_copy(x_way, way, s, c):
        return pltpu.make_async_remote_copy(
            src_ref=CP.at[x_way, s, c],
            dst_ref=CN.at[way, x_way, s, c],
            send_sem=ds_sem.at[x_way, way, s, c],
            recv_sem=dr_sem.at[x_way, way, s, c],
            device_id={"gx": beside[x_way], "gy": across[way]},
            device_id_type=MESH,
        )

    def exchange(s, c):
        copies = [d_copy(x_way, way, s, c) for x_way in (0, 1) for way in y_sides]
        copies += [y_copy(way, s, c) for way in y_sides]
        return copies + [x_copy(way, s, c) for way in (0, 1)]

    def ghost_exchange():
        copies = []
        for way in (0, 1):
            copies.append(
                pltpu.make_async_remote_copy(
                    src_ref=XSG.at[way],
                    dst_ref=XRG.at[way],
                    send_sem=gs_sem.at[way],
                    recv_sem=gr_sem.at[way],
                    device_id={"gx": beside[way]},
                    device_id_type=MESH,
                )
            )
        for way in y_sides:
            for i, e in enumerate((0, chunks + 1)):
                copies.append(
                    pltpu.make_async_remote_copy(
                        src_ref=YP.at[0, e, pl.ds(1, 2)],
                        dst_ref=YN.at[way, 0, e, pl.ds(1, 2)],
                        send_sem=gs_sem.at[2 + 2 * way + i],
                        recv_sem=gr_sem.at[2 + 2 * way + i],
                        device_id={"gy": across[way]},
                        device_id_type=MESH,
                    )
                )
        return copies

    def pack_high(first, second):
        return jnp.where(low, pltpu.roll(second, 4, 0), first)

    def pack_low(first, second):
        return jnp.where(low, first, pltpu.roll(second, 4, 0))

    def unpack_x(from_left, from_right):
        first = jnp.where(low, from_right, from_left)
        second = pltpu.roll(jnp.where(low, from_left, from_right), 4, 0)
        return first, second

    def pack_y(items):
        packed = None
        for k, item in enumerate(items):
            turned = jnp.where(first_half, pltpu.roll(item, 16 * k + 8, 1), pltpu.roll(item, 16 * k + 72, 1))
            packed = turned if packed is None else jnp.where(lane_group == k, turned, packed)
        return packed

    def by_side(values):
        return values[0] if ny == 2 else jnp.where(first_half, values[0], values[1])

    def both_edges(strip):
        return jnp.where(late, strip, pltpu.roll(strip, 64, 1))

    def place(edges, k, inner):
        return jnp.where(edge, pltpu.roll(edges, 128 - (16 * k + 8), 1), inner)

    def add(edges, k, inner):
        return inner + jnp.where(edge, pltpu.roll(edges, 128 - (16 * k + 8), 1), 0.0)

    def weighted(pairs):
        total = None
        for weight, (plus, minus) in zip(stencil, pairs, strict=True):
            term = weight * (plus - minus)
            total = term if total is None else total + term
        return total

    def band(items):
        flat = jnp.concatenate(items, axis=0) if isinstance(items, list) else items.reshape(-1, 128)
        high = flat.astype(jnp.bfloat16)
        rest = (flat - high.astype(jnp.float32)).astype(jnp.bfloat16)
        out = jnp.dot(jnp.concatenate([high, rest], axis=1), W[...], preferred_element_type=jnp.float32)
        return (out[:, :128] + out[:, 128:]).reshape(-1, 8, 128)

    def d_rows(ref, index, start):
        return weighted(
            [(ref[index + (pl.ds(start + s, 8),)], ref[index + (pl.ds(start - s, 8),)]) for s in range(1, 5)]
        )

    def d_x(field, halo):
        return weighted(
            [
                (
                    pltpu.roll(jnp.where(sub < s, halo, field), 8 - s, 0),
                    pltpu.roll(jnp.where(sub >= 8 - s, halo, field), s, 0),
                )
                for s in range(1, 5)
            ]
        )

    def d_z(ref, f, z):
        return weighted([(ref[f, z + s], ref[f, z - s]) for s in range(1, 5)])

    def tile(s, c, f, k):
        return XE[s, c + k // CH, HALF + CH * f + k % CH, OWN]

    def d_z_tile(s, c, f, k):
        return weighted([(tile(s, c, f, k + o), tile(s, c, f, k - o)) for o in range(1, 5)])

    def d_z_strip(s, c, f):
        values = []
        for way in y_sides:
            before, here, after = [YN[way, s, c + i, f] for i in range(3)]
            pairs = [
                (
                    pltpu.roll(jnp.where(lane_half < 16 * o, after, here), 128 - 16 * o, 1),
                    pltpu.roll(jnp.where(lane_half >= 64 - 16 * o, before, here), 16 * o, 1),
                )
                for o in range(1, 4)
            ]
            values.append(weighted(pairs + [(after, before)]))
        return by_side(values)

    def primitives(q):
        inverse = 1.0 / q[0]
        speeds = [q[1] * inverse, q[2] * inverse, q[3] * inverse]
        kinetic = 0.5 * (q[1] * speeds[0] + q[2] * speeds[1] + q[3] * speeds[2])
        pressure = 0.4 * (q[4] - kinetic)
        return speeds + [1.4 * pressure * inverse]

    def thermal(rho, v):
        m = [rho * v[i] for i in range(3)]
        p = (1.0 / 1.4) * (rho * v[3])
        total = 3.5 * p + 0.5 * (m[0] * v[0] + m[1] * v[1] + m[2] * v[2])
        return m, p, total

    def flux(along, v, state, stress, gradient):
        m, p, total = state
        out = [m[along]]
        for i in range(3):
            entry = m[i] * v[along] - stress[i]
            out.append(entry + p if i == along else entry)
        work = v[0] * stress[0] + v[1] * stress[1] + v[2] * stress[2] + conductivity * gradient
        out.append(total * v[along] - work)
        return out

    def shrink(gx, gy, gz):
        return (2.0 / 3.0 * viscosity) * (gx + gy + gz)

    def put(s, c, values):
        for f in range(4):
            for k in range(CH):
                XE[s, c, HALF + CH * f + k, OWN] = values[k][f]

    def prepare(s, c, values, rho):
        put(s, c + 2, values)
        for j in range(HALF):
            XE[s, c + 2, j, OWN] = pack_high(rho[j], rho[j + HALF])
            XE[s, c + 2, SENT + j, OWN] = pack_low(rho[j], rho[j + HALF])
        packs = [pack_y([values[k][f] for k in range(CH)]) for f in range(4)] + [pack_y(rho)]
        for f in range(5):
            YP[s, c + 1, f] = packs[f]
        corner = jnp.where(first_half, packs[0], packs[1])
        CP[0, s, c] = corner[4:]
        CP[1, s, c] = corner[:4]

    def start_chunk(c, carry):
        states = [[QE[f, GHOST + c * CH + k] for f in range(5)] for k in range(CH)]
        prepare(0, c, [primitives(q) for q in states], [q[0] for q in states])
        return carry

    def send_chunk(c, carry):
        for copy in exchange(0, c):
            copy.start()
        return carry

    def ghost_primitives(c):
        values = [primitives([QE[f, c * CH + k] for f in range(5)]) for k in range(CH)]
        for s in range(2):
            put(s, c, values)
        return values

    def ghost_start():
        near = []
        for e, c in ((0, 1), (chunks + 1, chunks + 2)):
            values = ghost_primitives(c)
            near += values
            for f in (1, 2):
                YP[0, e, f] = pack_y([values[k][f] for k in range(CH)])
        for i, f in enumerate((0, 2)):
            for k in range(4):
                XSG[0, i, k] = pack_high(near[k][f], near[k + 4][f])
                XSG[1, i, k] = pack_low(near[k][f], near[k + 4][f])

    def gradients_y(s):
        DY[...] = band(XE[s, pl.ds(2, chunks), pl.ds(HALF, 4 * CH), OWN]).reshape(DY.shape)

    def gradient_chunk(s, c, carry):
        for k in range(CH):
            for f in range(4):
                DZ[f, c * CH + k] = d_z_tile(s, c + 2, f, k)
        return carry

    def ghost_gradients():
        for copy in ghost_exchange():
            copy.wait_recv()
        sides = ((0, 0, 1), (chunks + 1, planes + 4, chunks + 2))
        items = []
        for e, _, c in sides:
            for f in (1, 2):
                for way in y_sides:
                    YN[way, 1, e, f] = YN[way, 0, e, f]
                merged = by_side([YN[way, 0, e, f] for way in y_sides])
                items.append(jnp.where(own_lane, YP[0, e, f], merged))
        for _, _, c in sides:
            items += [tile(0, c, f, k) for f in (1, 2) for k in range(CH)]
        out = band(items)
        for i, (_, at, c) in enumerate(sides):
            strips = [both_edges(out[2 * i + f]) for f in range(2)]
            inner = 4 + 2 * CH * i
            for k in range(CH):
                j = CH * i + k
                halos = []
                for n, f in enumerate((0, 2)):
                    halo = unpack_x(XRG[0, n, k], XRG[1, n, k])[i]
                    HH[f, at + k] = halo
                    halos.append(halo)
                GH[0, j] = d_x(tile(0, c, 0, k), halos[0]) + place(strips[0], k, out[inner + k])
                GH[1, j] = d_x(tile(0, c, 2, k), halos[1])
                GH[2, j] = place(strips[1], k, out[inner + CH + k])

    def ghost_flux(s):
        for e, at, c in ((0, 0, 1), (1, planes + 4, chunks + 2)):
            for k in range(CH):
                j = CH * e + k
                v = [tile(s, c, f, k) for f in range(4)]
                gz = [d_z_tile(s, c, f, k) for f in range(4)]
                dilation = (2.0 / 3.0 * viscosity) * (GH[0, j] + gz[2])
                stress = [
                    viscosity * (GH[1, j] + gz[0]),
                    viscosity * (GH[2, j] + gz[1]),
                    (2.0 * viscosity) * gz[2] - dilation,
                ]
                out = flux(2, v, thermal(QE[0, c * CH + k], v), stress, gz[3])
                for f in range(5):
                    FZ[f, at + k] = out[f]

    def beyond(s, c, f):
        return by_side([YN[way, s, c + 1, f] for way in y_sides])

    def corners(s, c):
        pairs = [jnp.concatenate([CN[way, 1, s, c], CN[way, 0, s, c]], axis=0) for way in y_sides]
        turned = [pltpu.roll(pair, 64, 1) for pair in pairs]
        first = [jnp.where(first_half, pair, turn) for pair, turn in zip(pairs, turned, strict=True)]
        second = [jnp.where(first_half, turn, pair) for pair, turn in zip(pairs, turned, strict=True)]
        return [by_side(first), by_side(second)]

    def arrive(s, c):
        for copy in exchange(s, c):
            copy.wait_recv()
        items = [jnp.where(own_lane, YP[s, c + 1, f], beyond(s, c, f)) for f in range(4)]
        items += [jnp.where(own_lane, 0.0, corner) for corner in corners(s, c)]
        for f in range(4):
            for k in range(CH):
                slot = HALF + CH * f + k
                halo = jnp.where(low, XE[s, c + 2, slot, AFTER], XE[s, c + 2, slot, BEFORE])
                HH[f, 4 + c * CH + k] = halo
                if f < 2:
                    items.append(halo)
        out = band(items)
        for f in range(4):
            SD[f, c] = out[f]
            ED[f, c] = both_edges(out[f])
        for f in range(2):
            HE[f, c] = both_edges(out[4 + f])
            for k in range(CH):
                HD[f, c * CH + k] = out[6 + CH * f + k]

    def strip_chunk(s, c):
        v = [beyond(s, c, f) for f in range(5)]
        strip_x = [d_x(v[f], corner) for f, corner in enumerate(corners(s, c))]
        strip_y = [SD[f, c] for f in range(4)]
        strip_z = [d_z_strip(s, c, f) for f in (1, 2)]
        dilation = shrink(strip_x[0], strip_y[1], strip_z[1])
        stress = [
            viscosity * (strip_x[1] + strip_y[0]),
            (2.0 * viscosity) * strip_y[1] - dilation,
            viscosity * (strip_y[2] + strip_z[0]),
        ]
        out = flux(1, v, thermal(v[4], v), stress, strip_y[3])
        out = band([jnp.where(own_lane, 0.0, out[min(f, 4)]) for f in range(6)])
        for f in range(5):
            RS[f, c] = both_edges(out[f])

    def halo_chunk(s, c):
        rho = [None] * CH
        for j in range(HALF):
            rho[j], rho[j + HALF] = unpack_x(XE[s, c + 2, j, BEFORE], XE[s, c + 2, SENT + j, AFTER])
        for k in range(CH):
            w = c * CH + k
            v = [HH[f, 4 + w] for f in range(4)]
            gx = [HX[f, w] for f in range(4)]
            gy = [add(HE[f, c], k, HD[f, w]) for f in range(2)]
            gz = [d_z(HH, f, 4 + w) for f in (0, 2)]
            dilation = shrink(gx[0], gy[1], gz[1])
            stress = [
                (2.0 * viscosity) * gx[0] - dilation,
                viscosity * (gx[1] + gy[0]),
                viscosity * (gx[2] + gz[0]),
            ]
            out = flux(0, v, thermal(rho[k], v), stress, gx[3])
            for f in range(5):
                FX[f, w, BEFORE] = out[f]
                FX[f, w, AFTER] = out[f]

    def flux_chunk(s, c):
        for k in range(CH):
            w = c * CH + k
            gx = []
            for f in range(4):
                index = (s, c + 2, HALF + CH * f + k)
                lower = d_rows(XE, index, 4)
                upper = d_rows(XE, index, 12)
                gx.append(pltpu.roll(jnp.where(low, upper, lower), 4, 0))
                HX[f, w] = pltpu.roll(jnp.where(low, lower, upper), 4, 0)
            v = [tile(s, c + 2, f, k) for f in range(4)]
            state = thermal(QE[0, GHOST + w], v)
            gy = [place(ED[f, c], k, DY[c, CH * f + k]) for f in range(4)]
            gz = [DZ[f, w] for f in range(4)]
            dilation = shrink(gx[0], gy[1], gz[2])
            txx = (2.0 * viscosity) * gx[0] - dilation
            tyy = (2.0 * viscosity) * gy[1] - dilation
            tzz = (2.0 * viscosity) * gz[2] - dilation
            txy = viscosity * (gx[1] + gy[0])
            txz = viscosity * (gx[2] + gz[0])
            tyz = viscosity * (gy[2] + gz[1])
            out_x = flux(0, v, state, [txx, txy, txz], gx[3])
            out_y = flux(1, v, state, [txy, tyy, tyz], gy[3])
            out_z = flux(2, v, state, [txz, tyz, tzz], gz[3])
            for f in range(5):
                FX[f, w, OWN] = out_x[f]
                FY[c, CH * f + k] = out_y[f]
                FZ[f, w + 4] = out_z[f]

    def update_chunk(s, c):
        inner = band(FY[c])
        values = []
        rho = []
        for k in range(CH):
            w = c * CH + k
            z = GHOST + w
            q = []
            for f in range(5):
                slope = d_rows(FX, (f, w), 8) + add(RS[f, c], k, inner[CH * f + k]) + d_z(FZ, f, w + 4)
                if s == 1:
                    slope_out[f, w] = slope - (section_a[1] / time_step) * REG[f, w]
                    continue
                register = section_a[0] * REG[f, w] - time_step * slope
                REG[f, w] = register
                state = QE[f, z] + section_b[0] * register
                QE[f, z] = state
                state_out[f, w] = state
                q.append(state)
            if s == 0:
                values.append(primitives(q))
                rho.append(q[0])
        if s == 0:
            prepare(1, c, values, rho)
            for copy in exchange(1, c):
                copy.start()

    def step(s, c):
        if c + 1 < chunks:
            arrive(s, c + 1)
            flux_chunk(s, c + 1)
        if c >= 0:
            strip_chunk(s, c)
            halo_chunk(s, c)
            update_chunk(s, c)

    offset = lax.broadcasted_iota(jnp.int32, (128, 128), 0) - lax.broadcasted_iota(jnp.int32, (128, 128), 1)
    distance = jnp.abs(offset)
    for weights, part in ((coarse, pl.ds(0, 128)), (fine, pl.ds(128, 128))):
        taps = jnp.zeros((128, 128), jnp.float32)
        for o, weight in enumerate(weights, start=1):
            taps = jnp.where(distance == o, weight, taps)
        taps = jnp.where(offset < 0, -taps, taps).astype(jnp.bfloat16)
        W[pl.ds(0, 128), part] = taps
        W[pl.ds(128, 128), part] = taps

    loads[0].wait()
    loads[1].wait()
    ghost_start()
    loads[2].wait()
    start_chunk(0, 0)
    pl.semaphore_wait(barrier, len(neighbours))
    for copy in ghost_exchange():
        copy.start()
    send_chunk(0, 0)
    for c in range(1, chunks):
        start_chunk(c, 0)
        send_chunk(c, 0)
    ghost_primitives(0)
    ghost_primitives(chunks + 3)
    for s in range(2):
        gradients_y(s)
        for c in range(chunks):
            gradient_chunk(s, c, 0)
        if s == 0:
            ghost_gradients()
            loads[3].wait()
        ghost_flux(s)
        for c in range(-1, chunks):
            step(s, c)

    for copy in ghost_exchange():
        copy.wait_send()

    def finish(c, carry):
        for s in range(2):
            for copy in exchange(s, c):
                copy.wait_send()
        return carry

    lax.fori_loop(0, chunks, finish, 0)


def solution(mesh):
    nx, ny = mesh.shape["gx"], mesh.shape["gy"]
    sides = 1 if ny == 2 else 2

    def body(conserved, register, ghost_planes):
        _, planes, rows, columns = conserved.shape
        assert (rows, columns) == (8, 128) and planes % CH == 0 and ghost_planes.shape[1] == 2 * GHOST
        chunks = planes // CH

        def vmem(*shape, rows=8):
            return pltpu.VMEM(shape + (rows, columns), jnp.float32)

        dma = pltpu.SemaphoreType.DMA
        state, slope = pl.pallas_call(
            functools.partial(kernel, nx, ny, chunks),
            out_shape=[pltpu.VMEM(conserved.shape, jnp.float32)] * 2,
            in_specs=[pl.BlockSpec(memory_space=pltpu.HBM)] * 3,
            out_specs=[pl.BlockSpec(memory_space=pltpu.VMEM)] * 2,
            scratch_shapes=[
                vmem(5, planes + 2 * GHOST),
                vmem(5, planes),
                vmem(2, chunks + 4, SLOTS, rows=24),
                vmem(2, chunks + 2, 5),
                vmem(sides, 2, chunks + 2, 5),
                vmem(2, 2, chunks, rows=4),
                vmem(sides, 2, 2, chunks, rows=4),
                vmem(4, planes + 8),
                vmem(2, 2, 4),
                vmem(2, 2, 4),
                vmem(chunks, 4 * CH),
                vmem(4, planes),
                vmem(5, planes, rows=24),
                vmem(chunks, 5 * CH),
                vmem(5, planes + 8),
                vmem(5, chunks),
                vmem(3, 8),
                vmem(4, chunks),
                vmem(4, chunks),
                vmem(2, chunks),
                vmem(2, planes),
                vmem(4, planes),
                pltpu.VMEM((256, 256), jnp.bfloat16),
                dma((4,)),
                dma((2, 2, chunks)),
                dma((2, 2, chunks)),
                dma((sides, 2, chunks)),
                dma((sides, 2, chunks)),
                dma((2, sides, 2, chunks)),
                dma((2, sides, 2, chunks)),
                dma((2 + 2 * sides,)),
                dma((2 + 2 * sides,)),
            ],
            compiler_params=pltpu.CompilerParams(
                collective_id=0, has_side_effects=True, vmem_limit_bytes=60 * 1024 * 1024
            ),
        )(conserved, register, ghost_planes)
        carried = -time_step * slope
        return state + section_b[1] * carried, carried

    spec = P(None, None, "gx", "gy")
    return jax.shard_map(
        body, mesh=mesh, in_specs=(spec, spec, spec), out_specs=(spec, spec), check_vma=False
    )
```
